512 devices in a mesh: pool: 64 (over x, z, core), tp: 8 (over y).
Axes of the slice: x: 4, y: 8, z: 8, core: 2. Of those that a mesh axis runs over, the one named last changes fastest.
Arguments:
- prefill_page_pool: bfloat16 [4096, 2, 64, 1024], P('pool', None, None, 'tp'), may hold values from -6 to 6
- prefill_page_table: int32 [2048, 2], P('pool'), may hold values from 0 to 63, as said below
- prefill_length: int32 [2048], P('pool'), may hold values from 1 to 128, as said below
- prefill_target_group: int32 [2048], P('pool'), may hold values from 0 to 63, as said below
- resident_page_pool: bfloat16 [1024, 2, 64, 1024], P('pool', None, None, 'tp'), may hold values from -6 to 6
- resident_page_table: int32 [512, 2], P('pool'), may hold values from 0 to 15, as said below
- resident_length: int32 [512], P('pool'), may hold values from 1 to 128, as said below
- tokens: bfloat16 [4608, 4, 5120], P('pool', None, 'tp'), may hold values from -6 to 6
- base_query_projection: bfloat16 [4608, 4, 4096], P('pool', None, 'tp'), may hold values from -6 to 6
- fresh_key_value: bfloat16 [4608, 4, 2, 1024], P('pool', None, None, 'tp'), may hold values from -6 to 6
- request_adapter: int32 [4608], P('pool'), may hold values from 0 to 511, as said below
- adapter_store_row: int32 [512], replicated, may hold values from 0 to 511
- shrink_weight: bfloat16 [512, 64, 5120], P('pool', None, 'tp'), may hold values from -0.078125 to 0.078125
- expand_weight: bfloat16 [512, 64, 4096], P('pool', None, 'tp'), may hold values from -0.75 to 0.75
Outputs:
- attn_out: bfloat16 [4608, 4, 4096], P('pool', None, 'tp')
The draws below stay inside these ranges and needn't reach their ends.
Inputs may be any that keep to these rules, and one draw needn't show every extreme that they name: `prefill_target_group`: the 32 requests of one prefill device go to distinct decode groups; at least one decode group receives a request from every prefill device, while other groups may have empty remote slots (arrived_len = 0). `prefill_page_table`: each prefill device's rows name each of its 64 pages once. `prefill_length`: every prefill device has a request of the largest length. `resident_page_table`: each decode group's rows name each of its 16 pages once. `resident_length`: every decode group has a resident request of the largest length. `request_adapter`: adapter_store_row is a permutation; the adapter in store row w is held by pool index w // 8. Among the 72 slots of one group at most 2 use adapters held by one pool index, and those use one adapter; in every group some pool index serves 2 slots.
All inputs are finite; a program needn't handle non-finite values.
Results may differ from the reference program's by a relative error of at most 0.02.
Values may be sent and summed in bfloat16 or wider, within the bound.
A program may use at most 128 MiB of HBM per device.

```python
import jax
import jax.numpy as jnp
from jax import lax

MODEL_WIDTH = 5120
KEY_VALUE_HEADS = 8
HEAD_WIDTH = 128
QUERY_HEAD_HALF = 32
ADAPTER_RANK = 64
PAGE_TOKENS = 64
PROMPT_PAGES = 2
RESIDENT_PAGES = 2
DECODE_STEPS = 4
OWNER_SLOT_ROWS = 2
ADP_DEV = 8
RESIDENT_REQUESTS = 8
PREFILL_REQUESTS = 32
GROUP_SLOTS = 72
ADAPTER_COUNT = 512
N_POOL = 64


def device_permutation(key, decode_group_count, length):
    sub_keys = jax.random.split(key, decode_group_count)
    return jax.vmap(lambda subkey: jax.random.permutation(subkey, length))(sub_keys).astype(jnp.int32)


def uneven_lengths(key, decode_group_count, per_group, longest):
    lengths = jax.random.randint(key, (decode_group_count, per_group), 1, longest + 1)
    full_spot = jax.random.randint(jax.random.fold_in(key, 1), (decode_group_count, 1), 0, per_group)
    lengths = jnp.where(jnp.arange(per_group)[None, :] == full_spot, longest, lengths)
    return lengths.reshape(-1).astype(jnp.int32)


def adapter_plan(key):
    decode_group_count = GROUP_SLOTS - RESIDENT_REQUESTS
    home_rows = jax.random.permutation(jax.random.fold_in(key, 101), decode_group_count * ADP_DEV).astype(jnp.int32)
    seat_index = device_permutation(jax.random.fold_in(key, 102), decode_group_count, OWNER_SLOT_ROWS * decode_group_count)[:, :GROUP_SLOTS]
    owner_ids = seat_index // OWNER_SLOT_ROWS
    local_ids = jax.random.randint(jax.random.fold_in(key, 103), (decode_group_count, decode_group_count), 0, ADP_DEV)
    row_ids = owner_ids * ADP_DEV + jnp.take_along_axis(local_ids, owner_ids, 1)
    inverse = jnp.argsort(home_rows).astype(jnp.int32)
    return (home_rows, inverse[row_ids].reshape(-1).astype(jnp.int32))


def draw_adapter_store_row(key, part):
    home_rows, chosen = adapter_plan(key)
    return home_rows


def draw_request_adapter(key, part):
    home_rows, chosen = adapter_plan(key)
    return chosen


def draw_prefill_target_group(key, part):
    key = jax.random.fold_in(key, 1)
    decode_group_count = GROUP_SLOTS - RESIDENT_REQUESTS
    busiest = jax.random.randint(jax.random.fold_in(key, 0), (), 0, decode_group_count)
    offsets = device_permutation(jax.random.fold_in(key, 1), decode_group_count, decode_group_count - 1)[:, :PREFILL_REQUESTS - 1] + 1
    offsets = jnp.concatenate([jnp.zeros((decode_group_count, 1), jnp.int32), offsets], 1)
    shuffle = device_permutation(jax.random.fold_in(key, 2), decode_group_count, PREFILL_REQUESTS)
    offsets = jnp.take_along_axis(offsets, shuffle, 1)
    return ((busiest + offsets) % decode_group_count).reshape(-1).astype(jnp.int32)


def draw_prefill_page_table(key, part):
    key = jax.random.fold_in(key, 2)
    decode_group_count = GROUP_SLOTS - RESIDENT_REQUESTS
    return device_permutation(key, decode_group_count, PREFILL_REQUESTS * PROMPT_PAGES).reshape(decode_group_count * PREFILL_REQUESTS, PROMPT_PAGES)


def draw_resident_page_table(key, part):
    key = jax.random.fold_in(key, 3)
    decode_group_count = GROUP_SLOTS - RESIDENT_REQUESTS
    return device_permutation(key, decode_group_count, RESIDENT_REQUESTS * RESIDENT_PAGES).reshape(decode_group_count * RESIDENT_REQUESTS, RESIDENT_PAGES)


def draw_prefill_length(key, part):
    key = jax.random.fold_in(key, 4)
    return uneven_lengths(key, GROUP_SLOTS - RESIDENT_REQUESTS, PREFILL_REQUESTS, PROMPT_PAGES * PAGE_TOKENS)


def draw_resident_length(key, part):
    key = jax.random.fold_in(key, 5)
    return uneven_lengths(key, GROUP_SLOTS - RESIDENT_REQUESTS, RESIDENT_REQUESTS, RESIDENT_PAGES * PAGE_TOKENS)


def draw_prefill_page_pool(key, part):
    key = jax.random.fold_in(key, 11)
    tensor_shape = ((GROUP_SLOTS - RESIDENT_REQUESTS) * PREFILL_REQUESTS * PROMPT_PAGES, 2, PAGE_TOKENS, KEY_VALUE_HEADS * HEAD_WIDTH)
    values = jnp.clip(jax.random.normal(key, tensor_shape, jnp.float32), -6.0, 6.0)
    return values.astype(jnp.bfloat16)


def draw_resident_page_pool(key, part):
    key = jax.random.fold_in(key, 12)
    tensor_shape = ((GROUP_SLOTS - RESIDENT_REQUESTS) * RESIDENT_REQUESTS * RESIDENT_PAGES, 2, PAGE_TOKENS, KEY_VALUE_HEADS * HEAD_WIDTH)
    values = jnp.clip(jax.random.normal(key, tensor_shape, jnp.float32), -6.0, 6.0)
    return values.astype(jnp.bfloat16)


def draw_base_query_projection(key, part):
    key = jax.random.fold_in(key, 13)
    total_row_count = (GROUP_SLOTS - RESIDENT_REQUESTS) * GROUP_SLOTS
    tensor_shape = (total_row_count, DECODE_STEPS, QUERY_HEAD_HALF * HEAD_WIDTH)
    values = jnp.clip(jax.random.normal(key, tensor_shape, jnp.float32), -6.0, 6.0)
    return values.astype(jnp.bfloat16)


def block_levels(own_key, shape, cuts, low, top_value):
    level = 1.0
    for axis_at, shards_of in cuts:
        draws = jax.random.uniform(jax.random.fold_in(jax.random.fold_in(own_key, 6), axis_at), (shards_of,), jnp.float32, low / len(cuts), top_value / len(cuts))
        level = level * jnp.repeat(jnp.exp(draws), shape[axis_at] // shards_of).reshape((-1,) + (1,) * (len(shape) - 1 - axis_at))
    return level


def normal_values(key, extent, spread, bound, cuts=(), held_as=jnp.bfloat16):
    loudness = block_levels(key, extent, cuts, -0.22, 0.18) if cuts else 1.0
    values = jax.random.normal(key, extent, jnp.float32) * spread * loudness
    return jnp.minimum(jnp.maximum(values, -bound), bound).astype(held_as)


def setup_inputs(seed: int = 0) -> dict:
    streams_of = jax.random.split(jax.random.key(seed), 15)
    prefill_page_pool = draw_prefill_page_pool(jax.random.fold_in(streams_of[14], 71), 0)
    prefill_page_table = draw_prefill_page_table(jax.random.fold_in(streams_of[14], 71), 0)
    prefill_length = draw_prefill_length(jax.random.fold_in(streams_of[14], 71), 0)
    prefill_target_group = draw_prefill_target_group(jax.random.fold_in(streams_of[14], 71), 0)
    resident_page_pool = draw_resident_page_pool(jax.random.fold_in(streams_of[14], 71), 0)
    resident_page_table = draw_resident_page_table(jax.random.fold_in(streams_of[14], 71), 0)
    resident_length = draw_resident_length(jax.random.fold_in(streams_of[14], 71), 0)
    tokens = normal_values(streams_of[7], (N_POOL * GROUP_SLOTS, DECODE_STEPS, MODEL_WIDTH), 1.0, 6.0, ((0, 64), (2, 8)))
    base_query_projection = draw_base_query_projection(jax.random.fold_in(streams_of[14], 71), 0)
    fresh_key_value = normal_values(streams_of[9], (N_POOL * GROUP_SLOTS, DECODE_STEPS, 2, KEY_VALUE_HEADS * HEAD_WIDTH), 1.0, 6.0, ((0, 64), (3, 8)))
    request_adapter = draw_request_adapter(jax.random.fold_in(streams_of[14], 71), 0)
    adapter_store_row = draw_adapter_store_row(jax.random.fold_in(streams_of[14], 71), 0)
    shrink_weight = normal_values(streams_of[12], (ADAPTER_COUNT, ADAPTER_RANK, MODEL_WIDTH), MODEL_WIDTH ** -0.5, 0.078125, ((0, 64), (2, 8)))
    expand_weight = normal_values(streams_of[13], (ADAPTER_COUNT, ADAPTER_RANK, QUERY_HEAD_HALF * HEAD_WIDTH), ADAPTER_RANK ** -0.5, 0.75, ((0, 64), (2, 8)))
    return dict(prefill_page_pool=prefill_page_pool, prefill_page_table=prefill_page_table, prefill_length=prefill_length, prefill_target_group=prefill_target_group, resident_page_pool=resident_page_pool, resident_page_table=resident_page_table, resident_length=resident_length, tokens=tokens, base_query_projection=base_query_projection, fresh_key_value=fresh_key_value, request_adapter=request_adapter, adapter_store_row=adapter_store_row, shrink_weight=shrink_weight, expand_weight=expand_weight)


def attend(queries, cache_pages, fresh_rows, lengths):
    number = queries.shape[0]
    decode_step_count = queries.shape[1]
    key_heads = cache_pages.shape[4] // HEAD_WIDTH
    shared = queries.shape[2] // (key_heads * HEAD_WIDTH)
    cached = cache_pages.shape[1] * cache_pages.shape[3]
    total_len = cached + decode_step_count
    keys_all = jnp.concatenate([cache_pages[:, :, 0].reshape(number, cached, -1), fresh_rows[:, :, 0]], 1)
    values_all = jnp.concatenate([cache_pages[:, :, 1].reshape(number, cached, -1), fresh_rows[:, :, 1]], 1)
    keys_all = keys_all.reshape(number, total_len, key_heads, HEAD_WIDTH).astype(jnp.float32)
    values_all = values_all.reshape(number, total_len, key_heads, HEAD_WIDTH).astype(jnp.float32)
    query_heads = queries.reshape(number, decode_step_count, key_heads, shared, HEAD_WIDTH).astype(jnp.float32)
    scores = jnp.einsum("nskgd,ntkd->nkgst", query_heads, keys_all) * (HEAD_WIDTH ** -0.5)
    position = jnp.arange(total_len, dtype=jnp.int32)[None, None, :]
    step_ids = jnp.arange(decode_step_count, dtype=jnp.int32)[None, :, None]
    visible = jnp.where(position < cached, position < lengths[:, None, None], position - cached <= step_ids)
    scores = jnp.where(visible[:, None, None], scores, -jnp.inf)
    highest = jnp.max(scores, axis=-1, keepdims=True)
    weights = jnp.exp(scores - highest)
    weights = (weights / jnp.sum(weights, axis=-1, keepdims=True)).astype(jnp.bfloat16)
    mixed_out = jnp.einsum("nkgst,ntkd->nskgd", weights.astype(jnp.float32), values_all)
    return mixed_out.reshape(number, decode_step_count, -1)


def reference(prefill_page_pool, prefill_page_table, prefill_length, prefill_target_group, resident_page_pool, resident_page_table, resident_length, tokens, base_query_projection, fresh_key_value, request_adapter, adapter_store_row, shrink_weight, expand_weight):
    every_page = prefill_page_pool.reshape(N_POOL, PREFILL_REQUESTS * PROMPT_PAGES, 2, PAGE_TOKENS, KEY_VALUE_HEADS * HEAD_WIDTH)
    tables = prefill_page_table.reshape(N_POOL, PREFILL_REQUESTS, PROMPT_PAGES)
    targets = prefill_target_group.reshape(N_POOL, PREFILL_REQUESTS)
    prompt_len = prefill_length.reshape(N_POOL, PREFILL_REQUESTS)
    resident_page_list = resident_page_pool.reshape(N_POOL, RESIDENT_REQUESTS * RESIDENT_PAGES, 2, PAGE_TOKENS, KEY_VALUE_HEADS * HEAD_WIDTH)
    res_tables = resident_page_table.reshape(N_POOL, RESIDENT_REQUESTS, RESIDENT_PAGES)
    res_lens = resident_length.reshape(N_POOL, RESIDENT_REQUESTS)
    token_row_block = tokens.reshape(N_POOL, GROUP_SLOTS, DECODE_STEPS, MODEL_WIDTH)
    base_query_rows = base_query_projection.reshape(N_POOL, GROUP_SLOTS, DECODE_STEPS, QUERY_HEAD_HALF * HEAD_WIDTH)
    fresh_tokens_all = fresh_key_value.reshape(N_POOL, GROUP_SLOTS, DECODE_STEPS, 2, KEY_VALUE_HEADS * HEAD_WIDTH)
    adapter_row_list = request_adapter.reshape(N_POOL, GROUP_SLOTS)
    sources = jnp.arange(N_POOL, dtype=jnp.int32)

    def one_group(decode_group_index):
        matched = targets == decode_group_index
        picked = jnp.sum(jnp.where(matched, jnp.arange(PREFILL_REQUESTS, dtype=jnp.int32)[None, :], 0), axis=1).astype(jnp.int32)
        arrived_len = jnp.sum(jnp.where(matched, prompt_len, 0), axis=1).astype(jnp.int32)
        arrived_table = jnp.take_along_axis(tables, picked[:, None, None], 1)[:, 0]
        arrived = every_page[sources[:, None], arrived_table]
        resident = resident_page_list[decode_group_index][res_tables[decode_group_index]]
        adapter_store_index = adapter_store_row[adapter_row_list[decode_group_index]]
        shrink_factor_rows = shrink_weight[adapter_store_index].astype(jnp.float32)
        rank_product = jnp.einsum("isd,ird->isr", token_row_block[decode_group_index].astype(jnp.float32), shrink_factor_rows).astype(jnp.bfloat16)
        rank_product = lax.optimization_barrier(rank_product)
        expand_factor_rows = expand_weight[adapter_store_index].astype(jnp.float32)
        adapter_delta = jnp.einsum("twf,tfn->twn", rank_product.astype(jnp.float32), expand_factor_rows).astype(jnp.bfloat16)
        adapter_delta = lax.optimization_barrier(adapter_delta)
        query_row_block = (base_query_rows[decode_group_index].astype(jnp.float32) + adapter_delta.astype(jnp.float32)).astype(jnp.bfloat16)
        fresh_group = fresh_tokens_all[decode_group_index]
        near_out = attend(query_row_block[:RESIDENT_REQUESTS], resident, fresh_group[:RESIDENT_REQUESTS], res_lens[decode_group_index])
        remote = attend(query_row_block[RESIDENT_REQUESTS:], arrived, fresh_group[RESIDENT_REQUESTS:], arrived_len)
        lengths = jnp.concatenate([res_lens[decode_group_index], arrived_len])
        mixed_out = jnp.concatenate([near_out, remote], 0)
        return jnp.where((lengths > 0)[:, None, None], mixed_out, 0.0).astype(jnp.bfloat16)

    attention_output = lax.map(one_group, sources)
    return attention_output.reshape(N_POOL * GROUP_SLOTS, DECODE_STEPS, QUERY_HEAD_HALF * HEAD_WIDTH)
```

```python
import jax
import jax.numpy as jnp
from jax import lax
from jax.sharding import PartitionSpec as P

HEAD_WIDTH = 128
SCALE = HEAD_WIDTH ** (-0.5)


def partial_attend(queries, keys, values, visible):
    scores = (
        jnp.einsum("nshd,ntd->nsht", queries, keys, preferred_element_type=jnp.float32) * SCALE
    )
    scores = jnp.where(visible[:, :, None, :], scores, -jnp.inf)
    highest = jnp.max(scores, axis=-1, keepdims=True)
    weights = jnp.exp(scores - highest)
    total = jnp.sum(weights, axis=-1, keepdims=True)
    mixed = jnp.einsum(
        "nsht,ntd->nshd", weights.astype(jnp.bfloat16), values, preferred_element_type=jnp.float32
    )
    return mixed / total, highest + jnp.log(total)


def body(
    prefill_page_pool,
    prefill_page_table,
    prefill_length,
    prefill_target_group,
    resident_page_pool,
    resident_page_table,
    resident_length,
    tokens,
    base_query_projection,
    fresh_key_value,
    request_adapter,
    adapter_store_row,
    shrink_weight,
    expand_weight,
):
    groups = lax.axis_size("pool")
    slots, steps, width = tokens.shape
    stored, rank, _ = shrink_weight.shape
    out_width = expand_weight.shape[2]
    heads = out_width // HEAD_WIDTH
    resident = resident_length.shape[0]
    per_owner = 2

    adapter_ids = jnp.arange(adapter_store_row.shape[0], dtype=jnp.int32)
    store_index = jnp.sum(
        jnp.where(request_adapter[:, None] == adapter_ids[None, :], adapter_store_row[None, :], 0),
        axis=1,
    )
    holder = store_index // stored
    within = store_index % stored
    slot_ids = jnp.arange(slots, dtype=jnp.int32)
    earlier = (holder[:, None] == holder[None, :]) & (slot_ids[None, :] < slot_ids[:, None])
    place = holder * per_owner + jnp.sum(earlier.astype(jnp.int32), axis=1)
    places = groups * per_owner
    dispatch = (jnp.arange(places, dtype=jnp.int32)[:, None] == place[None, :]).astype(jnp.bfloat16)
    owned_by = holder[:, None] == jnp.arange(groups, dtype=jnp.int32)[None, :]
    wanted = jnp.max(jnp.where(owned_by, within[:, None], 0), axis=0)

    asked = lax.all_to_all(wanted[:, None], "pool", 0, 0, tiled=True)[:, 0]
    outgoing = jnp.dot(
        dispatch, tokens.reshape(slots, steps * width), preferred_element_type=jnp.float32
    ).astype(jnp.bfloat16)
    visiting = lax.all_to_all(outgoing, "pool", 0, 0, tiled=True)
    rows = places * steps
    visiting = visiting.reshape(rows, width)
    which = jnp.repeat(asked, per_owner * steps)
    chosen = which[:, None] == jnp.arange(stored * rank, dtype=jnp.int32)[None, :] // rank
    every = lax.dot_general(
        visiting,
        shrink_weight.reshape(stored * rank, width),
        (((1,), (1,)), ((), ())),
        preferred_element_type=jnp.float32,
    )
    low = jnp.sum(jnp.where(chosen, every, 0.0).reshape(rows, stored, rank), axis=1)
    low = lax.psum(low.astype(jnp.bfloat16), "tp")
    spread = jnp.where(chosen, jnp.tile(low, (1, stored)), 0)
    delta = jnp.dot(
        spread, expand_weight.reshape(stored * rank, out_width), preferred_element_type=jnp.float32
    ).astype(jnp.bfloat16)
    delta = lax.all_to_all(
        delta.reshape(places, steps * out_width), "pool", 0, 0, tiled=True
    )
    delta = lax.dot_general(
        dispatch, delta, (((0,), (0,)), ((), ())), preferred_element_type=jnp.float32
    )
    query = (
        base_query_projection.astype(jnp.float32) + delta.reshape(slots, steps, out_width)
    ).astype(jnp.bfloat16)

    arrived = lax.all_to_all(query[resident:], "pool", 0, 0, tiled=True)
    arrived = arrived[prefill_target_group].reshape(-1, steps, heads, HEAD_WIDTH)
    pages = prefill_page_pool[prefill_page_table]
    cached = pages.shape[1] * pages.shape[3]
    position = jnp.arange(cached, dtype=jnp.int32)[None, None, :]
    keys = pages[:, :, 0].reshape(-1, cached, HEAD_WIDTH)
    values = pages[:, :, 1].reshape(-1, cached, HEAD_WIDTH)
    mixed, level = partial_attend(
        arrived, keys, values, position < prefill_length[:, None, None]
    )
    number = mixed.shape[0]
    back = (
        jnp.zeros((groups, steps * out_width), jnp.bfloat16)
        .at[prefill_target_group]
        .set(mixed.astype(jnp.bfloat16).reshape(number, -1))
    )
    back_level = (
        jnp.full((groups, steps * heads), -jnp.inf, jnp.float32)
        .at[prefill_target_group]
        .set(level.reshape(number, -1))
    )
    back = lax.all_to_all(back, "pool", 0, 0, tiled=True)
    back_level = lax.all_to_all(back_level, "pool", 0, 0, tiled=True)

    query = query.reshape(slots, steps, heads, HEAD_WIDTH)
    own_pages = resident_page_pool[resident_page_table]
    own_mixed, own_level = partial_attend(
        query[:resident],
        own_pages[:, :, 0].reshape(-1, cached, HEAD_WIDTH),
        own_pages[:, :, 1].reshape(-1, cached, HEAD_WIDTH),
        position < resident_length[:, None, None],
    )
    step_ids = jnp.arange(steps, dtype=jnp.int32)
    fresh_mixed, fresh_level = partial_attend(
        query,
        fresh_key_value[:, :, 0],
        fresh_key_value[:, :, 1],
        (step_ids[None, :] <= step_ids[:, None])[None],
    )
    cache_mixed = jnp.concatenate(
        [own_mixed, back.reshape(-1, steps, heads, HEAD_WIDTH).astype(jnp.float32)], 0
    )
    cache_level = jnp.concatenate(
        [own_level, back_level.reshape(-1, steps, heads, 1)], 0
    )
    top = jnp.maximum(cache_level, fresh_level)
    cache_share = jnp.exp(cache_level - top)
    fresh_share = jnp.exp(fresh_level - top)
    result = (cache_share * cache_mixed + fresh_share * fresh_mixed) / (cache_share + fresh_share)
    result = jnp.where(cache_level > -jnp.inf, result, 0.0)
    return result.reshape(slots, steps, out_width).astype(jnp.bfloat16)


def solution(mesh):
    return jax.shard_map(
        body,
        mesh=mesh,
        in_specs=(
            P("pool", None, None, "tp"),
            P("pool", None),
            P("pool"),
            P("pool"),
            P("pool", None, None, "tp"),
            P("pool", None),
            P("pool"),
            P("pool", None, "tp"),
            P("pool", None, "tp"),
            P("pool", None, None, "tp"),
            P("pool"),
            P(),
            P("pool", None, "tp"),
            P("pool", None, "tp"),
        ),
        out_specs=P("pool", None, "tp"),
        check_vma=False,
    )
```

```python
import jax
import jax.numpy as jnp
from jax import lax
from jax.experimental import pallas as pl
from jax.experimental.pallas import tpu as pltpu
from jax.sharding import PartitionSpec as P

HEAD_WIDTH = 128
SCALE = HEAD_WIDTH ** (-0.5)
MESH = pl.DeviceIdType.MESH
PER_OWNER = 2
CORES = 2
Z_CHIPS = 8
CHUNK = 16


def kernel(
    page0_ref,
    page1_ref,
    length_ref,
    own_table_ref,
    own_length_ref,
    request_ref,
    store_row_ref,
    tokens_ref,
    shrink_hbm,
    expand_hbm,
    base_hbm,
    fresh_hbm,
    pages_hbm,
    own_pages_hbm,
    out_ref,
    shrink_ref,
    expand_ref,
    base_ref,
    fresh_ref,
    pages_ref,
    own_pages_ref,
    gather_ref,
    x_send,
    x_recv,
    pick_send,
    pick_recv,
    part_send,
    part_recv,
    delta_send,
    delta_recv,
    fresh_recv,
    query_ref,
    query_recv,
    mixed_send,
    own_mixed,
    score_ref,
    weight_ref,
    mix_ref,
    load_sem,
    x_sem,
    pick_sem,
    part_sem,
    query_sem,
    one_sem,
    send_sem,
):
    groups = x_send.shape[0]
    peers = lax.axis_size("tp")
    slots = base_ref.shape[0]
    resident = own_length_ref.shape[0]
    steps = 4
    block = PER_OWNER * steps
    chunk = min(CHUNK, groups)
    chunks = groups // chunk
    rank = 64
    me = lax.axis_index("pool")
    row = lax.axis_index("tp")
    z_chips = min(Z_CHIPS, groups // CORES)
    x_chips = groups // (z_chips * CORES)
    my_x, my_z, my_core = me // (z_chips * CORES), (me // CORES) % z_chips, me % CORES

    def partner(k, sign):
        at_x, at, at_core = k // (z_chips * CORES), (k // CORES) % z_chips, k % CORES
        odd = at % 2
        at_z = odd * ((at + 1) // 2) + (1 - odd) * ((z_chips - at // 2) % z_chips)
        if sign < 0:
            at_x, at_z, at_core = x_chips - at_x, z_chips - at_z, CORES - at_core
        to_x = lax.rem(my_x + at_x, x_chips)
        to_z = lax.rem(my_z + at_z, z_chips)
        to_core = lax.rem(my_core + at_core, CORES)
        return (to_x * z_chips + to_z) * CORES + to_core

    barrier = pltpu.get_barrier_semaphore()

    @pl.loop(1, groups)
    def _(k):
        pl.semaphore_signal(
            barrier, inc=1, device_id={"pool": partner(k, 1)}, device_id_type=MESH
        )

    @pl.loop(1, peers)
    def _(j):
        pl.semaphore_signal(
            barrier, inc=1, device_id={"tp": lax.rem(row + j, peers)}, device_id_type=MESH
        )

    loads = [
        pltpu.make_async_copy(source, target, load_sem.at[n])
        for n, (source, target) in enumerate(
            [
                (shrink_hbm, shrink_ref),
                (expand_hbm, expand_ref),
                (base_hbm, base_ref),
                (fresh_hbm, fresh_ref),
                (pages_hbm, pages_ref),
                (own_pages_hbm, own_pages_ref),
            ]
        )
    ]
    for load in loads:
        load.start()

    stored = shrink_ref.shape[0] // rank
    adapters = store_row_ref.shape[1]
    store_row = store_row_ref[...]
    request = request_ref[...]
    half = lax.broadcasted_iota(jnp.int32, (8, adapters), 0)
    parts = jnp.where(half == 0, store_row // stored, store_row % stored)
    named = lax.broadcasted_iota(jnp.int32, (adapters, slots), 0) == request
    found = jnp.dot(
        parts.astype(jnp.float32).astype(jnp.bfloat16),
        jnp.where(named, 1.0, 0.0).astype(jnp.bfloat16),
        preferred_element_type=jnp.float32,
    )
    holder, within = found[0:1], found[1:2]
    slot_row = lax.broadcasted_iota(jnp.int32, (slots, slots), 0)
    slot_col = lax.broadcasted_iota(jnp.int32, (slots, slots), 1)
    holder_col = jnp.sum(
        jnp.where(slot_row == slot_col, holder, 0.0), axis=1, keepdims=True
    )
    earlier = (holder_col == holder) & (slot_row < slot_col)
    place = holder * PER_OWNER + jnp.sum(
        jnp.where(earlier, 1.0, 0.0), axis=0, keepdims=True
    )

    holder_ids = lax.broadcasted_iota(jnp.int32, (groups, slots), 0).astype(jnp.float32)
    wanted = jnp.max(jnp.where(holder_ids == holder, within, 0.0), axis=1, keepdims=True)
    pick_send[...] = jnp.broadcast_to(wanted, (groups, HEAD_WIDTH)).reshape(
        groups, 1, HEAD_WIDTH
    )

    wide = slots * steps
    widen = lax.broadcasted_iota(
        jnp.int32, (slots, wide), 1
    ) // steps == lax.broadcasted_iota(jnp.int32, (slots, wide), 0)
    place_wide = jnp.dot(
        jnp.broadcast_to(place, (8, slots)).astype(jnp.bfloat16),
        jnp.where(widen, 1.0, 0.0).astype(jnp.bfloat16),
        preferred_element_type=jnp.float32,
    )[0:1]
    step_of = lax.broadcasted_iota(jnp.int32, (1, wide), 1) % steps
    place_wide = place_wide * steps + step_of.astype(jnp.float32)
    row_ids = lax.broadcasted_iota(jnp.int32, (groups * block, wide), 0).astype(jnp.float32)
    dispatch = jnp.where(row_ids == place_wide, 1.0, 0.0).astype(jnp.bfloat16)
    outgoing = jnp.dot(dispatch, tokens_ref[...], preferred_element_type=jnp.float32)
    x_send[...] = outgoing.reshape(x_send.shape).astype(jnp.bfloat16)

    pl.semaphore_wait(barrier, groups - 1 + peers - 1)

    @pl.loop(1, groups)
    def _(k):
        to = partner(k, -1)
        pltpu.make_async_remote_copy(
            x_send.at[to],
            x_recv.at[k],
            send_sem.at[0],
            x_sem.at[k // chunk],
            device_id={"pool": to},
            device_id_type=MESH,
        ).start()
        pltpu.make_async_remote_copy(
            pick_send.at[to],
            pick_recv.at[k],
            send_sem.at[1],
            pick_sem.at[k // chunk],
            device_id={"pool": to},
            device_id_type=MESH,
        ).start()

    pltpu.make_async_copy(x_send.at[me], x_recv.at[0], x_sem.at[0]).start()
    pltpu.make_async_copy(pick_send.at[me], pick_recv.at[0], pick_sem.at[0]).start()

    span = slots * block
    line = lax.broadcasted_iota(jnp.int32, (span, slots), 0)
    own_line = line // block == lax.broadcasted_iota(jnp.int32, (span, slots), 1)
    holder_line = jnp.sum(jnp.where(own_line, holder, 0.0), axis=1, keepdims=True)
    place_line = jnp.sum(jnp.where(own_line, place, 0.0), axis=1, keepdims=True)
    inner = lax.broadcasted_iota(jnp.int32, (span, 1), 0) % block
    inner = (inner // steps) * block + inner % steps
    source = (
        holder_line * (2 * block)
        + (place_line - holder_line * PER_OWNER) * steps
        + inner.astype(jnp.float32)
    )
    column = lax.broadcasted_iota(jnp.int32, (span, groups * 2 * block), 1)
    gather_ref[...] = jnp.where(column.astype(jnp.float32) == source, 1.0, 0.0).astype(
        jnp.bfloat16
    )

    loads[0].wait()
    loads[1].wait()
    lanes = HEAD_WIDTH // rank
    rows = chunk * block
    tiles = stored // lanes
    lane = lax.broadcasted_iota(jnp.int32, (rows, HEAD_WIDTH), 1)
    lane_half = (lane // rank).astype(jnp.float32)
    low_lane = lax.broadcasted_iota(jnp.int32, (rows // 2, HEAD_WIDTH), 1) < rank

    def wait_for(ref, sem):
        pltpu.make_async_copy(ref, ref, sem).wait()

    def picked(c):
        pick = pick_recv[pl.ds(c * chunk, chunk)]
        return jnp.broadcast_to(pick, (chunk, block, HEAD_WIDTH)).reshape(rows, HEAD_WIDTH)

    def shrink_chunk(c):
        here = pl.ds(c * chunk, chunk)
        wait_for(x_recv.at[here], x_sem.at[c])
        wait_for(pick_recv.at[here], pick_sem.at[c])
        x = x_recv[here].reshape(rows, x_recv.shape[2])
        every = lax.dot_general(
            x, shrink_ref[...], (((1,), (1,)), ((), ())), preferred_element_type=jnp.float32
        )
        pick = picked(c)
        low = jnp.zeros((rows, HEAD_WIDTH), jnp.float32)
        for tile in range(tiles):
            part = every[:, tile * HEAD_WIDTH : (tile + 1) * HEAD_WIDTH]
            low += jnp.where(pick == lane_half + tile * lanes, part, 0.0)
        low += pltpu.roll(low, rank, 1)
        part_send[c] = jnp.where(low_lane, low[: rows // 2], low[rows // 2 :]).astype(
            jnp.bfloat16
        )
        pltpu.make_async_copy(
            part_send.at[c], part_recv.at[c, row], part_sem.at[c]
        ).start()

        @pl.loop(1, peers)
        def _(j):
            pltpu.make_async_remote_copy(
                part_send.at[c],
                part_recv.at[c, row],
                send_sem.at[2],
                part_sem.at[c],
                device_id={"tp": lax.rem(row + j, peers)},
                device_id_type=MESH,
            ).start()

    def expand_chunk(c):
        wait_for(part_recv.at[c], part_sem.at[c])
        total = jnp.sum(part_recv[c].astype(jnp.float32), axis=0)
        total = total.astype(jnp.bfloat16).astype(jnp.float32)
        turned = pltpu.roll(total, rank, 1)
        low = jnp.concatenate(
            [jnp.where(low_lane, total, turned), jnp.where(low_lane, turned, total)], 0
        )
        pick = picked(c)
        spread = jnp.concatenate(
            [jnp.where(pick == lane_half + tile * lanes, low, 0.0) for tile in range(tiles)], 1
        ).astype(jnp.bfloat16)
        delta = jnp.dot(spread, expand_ref[...], preferred_element_type=jnp.float32)
        here = pl.ds(c * chunk, chunk)
        for head in range(4):
            piece = delta[:, head * HEAD_WIDTH : (head + 1) * HEAD_WIDTH]
            delta_send[here, head * block : (head + 1) * block, :] = piece.reshape(
                chunk, block, HEAD_WIDTH
            ).astype(jnp.bfloat16)

        @pl.loop(c * chunk, (c + 1) * chunk)
        def _(k):
            @pl.when(k > 0)
            def _():
                pltpu.make_async_remote_copy(
                    delta_send.at[k],
                    delta_recv.at[me],
                    send_sem.at[3],
                    one_sem.at[0],
                    device_id={"pool": partner(k, 1)},
                    device_id_type=MESH,
                ).start()

    shrink_chunk(0)

    @pl.loop(1, chunks)
    def _(c):
        shrink_chunk(c)
        expand_chunk(c - 1)

    expand_chunk(chunks - 1)
    pltpu.make_async_copy(delta_send.at[0], delta_recv.at[me], one_sem.at[0]).start()

    loads[3].wait()

    @pl.loop(1, groups)
    def _(k):
        to = partner(k, -1)
        pltpu.make_async_remote_copy(
            fresh_ref.at[resident + to],
            fresh_recv.at[k],
            send_sem.at[4],
            one_sem.at[1],
            device_id={"pool": to},
            device_id_type=MESH,
        ).start()

    pltpu.make_async_copy(fresh_ref.at[resident + me], fresh_recv.at[0], one_sem.at[1]).start()
    loads[2].wait()
    loads[4].wait()
    loads[5].wait()

    wait_for(delta_recv, one_sem.at[0])
    for pair in range(2):
        here = slice(pair * 2 * block, (pair + 1) * 2 * block)
        delta = jnp.dot(
            gather_ref[...],
            delta_recv[:, here, :].reshape(groups * 2 * block, HEAD_WIDTH),
            preferred_element_type=jnp.float32,
        ).reshape(slots, block, HEAD_WIDTH)
        mine = slice(pair * block, (pair + 1) * block)
        query_ref[:, mine, :] = (base_ref[:, mine, :].astype(jnp.float32) + delta).astype(
            jnp.bfloat16
        )

    @pl.loop(1, groups)
    def _(k):
        to = partner(k, -1)
        pltpu.make_async_remote_copy(
            query_ref.at[resident + to],
            query_recv.at[k],
            send_sem.at[5],
            query_sem.at[k // chunk],
            device_id={"pool": to},
            device_id_type=MESH,
        ).start()

    pltpu.make_async_copy(
        query_ref.at[resident + me], query_recv.at[0], query_sem.at[0]
    ).start()

    def attend(number, queries, fresh, slot_pages, slot_length, pool_ref):
        lines = number * 16
        flat = queries.reshape(lines, HEAD_WIDTH)
        new = fresh.reshape(-1, HEAD_WIDTH)
        new_scores = (
            lax.dot_general(
                flat, new, (((1,), (1,)), ((), ())), preferred_element_type=jnp.float32
            )
            * SCALE
        )
        at = lax.broadcasted_iota(jnp.int32, new_scores.shape, 0)
        key = lax.broadcasted_iota(jnp.int32, new_scores.shape, 1)
        seen = (at // 16 == key // 8) & ((key % 8) // 2 <= at % steps) & (key % 2 == 0)
        new_scores = jnp.where(seen, new_scores, -jnp.inf)
        position = lax.broadcasted_iota(jnp.int32, (16, HEAD_WIDTH), 1)
        for m in range(number):
            first, second = slot_pages(m)
            keys = jnp.concatenate([pool_ref[first, 0], pool_ref[second, 0]], 0)
            scores = lax.dot_general(
                queries[m], keys, (((1,), (1,)), ((), ())), preferred_element_type=jnp.float32
            )
            score_ref[m * 16 : (m + 1) * 16, :] = jnp.where(
                position < slot_length(m), scores * SCALE, -jnp.inf
            )
        scores = score_ref[:lines, :]
        highest = jnp.maximum(
            jnp.max(scores, axis=1, keepdims=True), jnp.max(new_scores, axis=1, keepdims=True)
        )
        weights = jnp.exp(scores - highest)
        new_weights = jnp.exp(new_scores - highest)
        total = jnp.sum(weights, axis=1, keepdims=True) + jnp.sum(
            new_weights, axis=1, keepdims=True
        )
        weight_ref[:lines, :] = weights.astype(jnp.bfloat16)
        for m in range(number):
            first, second = slot_pages(m)
            values = jnp.concatenate([pool_ref[first, 1], pool_ref[second, 1]], 0)
            mixed = jnp.dot(
                weight_ref[m * 16 : (m + 1) * 16, :], values, preferred_element_type=jnp.float32
            )
            mix_ref[m * 16 : (m + 1) * 16, :] = jnp.where(slot_length(m) > 0, mixed, 0.0)
        moved = pltpu.roll(new_weights, 1, 1).astype(jnp.bfloat16)
        new_mixed = jnp.dot(moved, new, preferred_element_type=jnp.float32)
        return (mix_ref[:lines, :] + new_mixed) / total

    own = attend(
        resident,
        query_ref[:resident],
        fresh_ref[:chunk],
        lambda m: (own_table_ref[m, 0], own_table_ref[m, 1]),
        lambda m: own_length_ref[m],
        own_pages_ref,
    )
    own_mixed[...] = own.reshape(own_mixed.shape).astype(jnp.bfloat16)
    own_copy = pltpu.make_async_copy(own_mixed, out_ref.at[pl.ds(0, resident)], one_sem.at[3])
    own_copy.start()

    wait_for(fresh_recv, one_sem.at[1])

    @pl.loop(0, chunks)
    def _(c):
        here = pl.ds(c * chunk, chunk)
        wait_for(query_recv.at[here], query_sem.at[c])
        at = [partner(c * chunk + m, 1) for m in range(chunk)]
        mixed = attend(
            chunk,
            query_recv[here],
            fresh_recv[here],
            lambda m: (page0_ref[at[m]], page1_ref[at[m]]),
            lambda m: length_ref[at[m]],
            pages_ref,
        ).reshape(chunk, 16, HEAD_WIDTH)
        for m in range(chunk):
            mixed_send[c * chunk + m] = jnp.where(length_ref[at[m]] > 0, mixed[m], 0.0).astype(
                jnp.bfloat16
            )

        @pl.loop(c * chunk, (c + 1) * chunk)
        def _(k):
            @pl.when(k > 0)
            def _():
                pltpu.make_async_remote_copy(
                    mixed_send.at[k],
                    out_ref.at[resident + me],
                    send_sem.at[6],
                    one_sem.at[2],
                    device_id={"pool": partner(k, 1)},
                    device_id_type=MESH,
                ).start()

    pltpu.make_async_copy(
        mixed_send.at[0], out_ref.at[resident + me], one_sem.at[2]
    ).start()

    others = pl.ds(0, groups - 1)
    wait_for(x_send.at[others], send_sem.at[0])
    wait_for(pick_send.at[others], send_sem.at[1])
    wait_for(part_recv.at[:, pl.ds(0, peers - 1)], send_sem.at[2])
    wait_for(delta_send.at[others], send_sem.at[3])
    wait_for(fresh_recv.at[others], send_sem.at[4])
    wait_for(query_recv.at[others], send_sem.at[5])
    wait_for(mixed_send.at[others], send_sem.at[6])
    own_copy.wait()
    wait_for(mixed_send, one_sem.at[2])


def body(
    prefill_page_pool,
    prefill_page_table,
    prefill_length,
    prefill_target_group,
    resident_page_pool,
    resident_page_table,
    resident_length,
    tokens,
    base_query_projection,
    fresh_key_value,
    request_adapter,
    adapter_store_row,
    shrink_weight,
    expand_weight,
):
    groups = lax.axis_size("pool")
    peers = lax.axis_size("tp")
    slots, steps, width = tokens.shape
    stored, rank, _ = shrink_weight.shape
    out_width = expand_weight.shape[2]
    heads = out_width // HEAD_WIDTH
    resident = resident_length.shape[0]
    block = PER_OWNER * steps
    lines = heads * steps
    chunk = min(CHUNK, groups)
    chunks = groups // chunk

    group_ids = jnp.arange(groups, dtype=jnp.int32)
    meant = prefill_target_group[:, None] == group_ids[None, :]
    page0 = jnp.sum(jnp.where(meant, prefill_page_table[:, 0:1], 0), axis=0)
    page1 = jnp.sum(jnp.where(meant, prefill_page_table[:, 1:2], 0), axis=0)
    length = jnp.sum(jnp.where(meant, prefill_length[:, None], 0), axis=0)
    base = (
        base_query_projection.reshape(slots, steps, heads, HEAD_WIDTH)
        .transpose(0, 2, 1, 3)
        .reshape(slots, lines, HEAD_WIDTH)
    )
    operands = [
        page0,
        page1,
        length,
        resident_page_table,
        resident_length,
        request_adapter.reshape(1, slots),
        adapter_store_row.reshape(1, -1),
        tokens.reshape(slots * steps, width),
        shrink_weight.reshape(stored * rank, width),
        expand_weight.reshape(stored * rank, out_width),
        base,
        fresh_key_value.reshape(slots, 2 * steps, HEAD_WIDTH),
        prefill_page_pool,
        resident_page_pool,
    ]
    smem = pl.BlockSpec(memory_space=pltpu.SMEM)
    vmem = pl.BlockSpec(memory_space=pltpu.VMEM)
    hbm = pl.BlockSpec(memory_space=pl.ANY)
    half = jnp.bfloat16
    dma = pltpu.SemaphoreType.DMA
    out = pl.pallas_call(
        kernel,
        out_shape=jax.ShapeDtypeStruct((slots, lines, HEAD_WIDTH), half),
        in_specs=[smem] * 5 + [vmem] * 3 + [hbm] * 6,
        out_specs=hbm,
        scratch_shapes=[
            pltpu.VMEM(operand.shape, half) for operand in operands[8:]
        ]
        + [
            pltpu.VMEM((slots * block, groups * 2 * block), half),
            pltpu.VMEM((groups, block, width), half),
            pltpu.VMEM((groups, block, width), half),
            pltpu.VMEM((groups, 1, HEAD_WIDTH), jnp.float32),
            pltpu.VMEM((groups, 1, HEAD_WIDTH), jnp.float32),
            pltpu.VMEM((chunks, chunk * block // 2, HEAD_WIDTH), half),
            pltpu.VMEM((chunks, peers, chunk * block // 2, HEAD_WIDTH), half),
            pltpu.VMEM((groups, heads * block, HEAD_WIDTH), half),
            pltpu.VMEM((groups, heads * block, HEAD_WIDTH), half),
            pltpu.VMEM((groups, 2 * steps, HEAD_WIDTH), half),
            pltpu.VMEM((slots, lines, HEAD_WIDTH), half),
            pltpu.VMEM((groups, lines, HEAD_WIDTH), half),
            pltpu.VMEM((groups, lines, HEAD_WIDTH), half),
            pltpu.VMEM((resident, lines, HEAD_WIDTH), half),
            pltpu.VMEM((chunk * lines, HEAD_WIDTH), jnp.float32),
            pltpu.VMEM((chunk * lines, HEAD_WIDTH), half),
            pltpu.VMEM((chunk * lines, HEAD_WIDTH), jnp.float32),
            dma((6,)),
            dma((chunks,)),
            dma((chunks,)),
            dma((chunks,)),
            dma((chunks,)),
            dma((4,)),
            dma((7,)),
        ],
        compiler_params=pltpu.CompilerParams(
            collective_id=0, has_side_effects=True, vmem_limit_bytes=48 * 1024 * 1024
        ),
    )(*operands)
    return (
        out.reshape(slots, heads, steps, HEAD_WIDTH)
        .transpose(0, 2, 1, 3)
        .reshape(slots, steps, out_width)
    )


def solution(mesh):
    return jax.shard_map(
        body,
        mesh=mesh,
        in_specs=(
            P("pool", None, None, "tp"),
            P("pool", None),
            P("pool"),
            P("pool"),
            P("pool", None, None, "tp"),
            P("pool", None),
            P("pool"),
            P("pool", None, "tp"),
            P("pool", None, "tp"),
            P("pool", None, None, "tp"),
            P("pool"),
            P(),
            P("pool", None, "tp"),
            P("pool", None, "tp"),
        ),
        out_specs=P("pool", None, "tp"),
        check_vma=False,
    )
```

```python
import functools

import jax
import jax.numpy as jnp
from jax import lax
from jax.experimental import pallas as pl
from jax.experimental.pallas import tpu as pltpu
from jax.sharding import PartitionSpec as P

HEAD_WIDTH = 128
SCALE = HEAD_WIDTH ** (-0.5)
MESH = pl.DeviceIdType.MESH
PER_OWNER = 2
CORES = 2
Z_CHIPS = 8
FRESH_SLOTS = HEAD_WIDTH // 8


def kernel(
    target_hbm,
    length_hbm,
    table_hbm,
    own_length_hbm,
    own_table_hbm,
    request_hbm,
    store_row_hbm,
    tokens_hbm,
    shrink_hbm,
    expand_hbm,
    base_hbm,
    fresh_hbm,
    pages_hbm,
    own_pages_hbm,
    out_ref,
    target_ref,
    length_ref,
    table_ref,
    own_length_ref,
    own_table_ref,
    request_ref,
    store_row_ref,
    tokens_ref,
    shrink_ref,
    expand_ref,
    base_ref,
    fresh_ref,
    pages_ref,
    own_pages_ref,
    plan_line,
    plan_ref,
    gather_ref,
    x_send,
    x_recv,
    pick_send,
    pick_recv,
    part_send,
    part_recv,
    delta_send,
    delta_recv,
    fresh_recv,
    query_ref,
    query_recv,
    mixed_send,
    own_mixed,
    score_ref,
    weight_ref,
    mix_ref,
    load_sem,
    x_sem,
    pick_sem,
    part_sem,
    query_sem,
    one_sem,
    send_sem,
):
    groups = x_send.shape[0]
    peers = lax.axis_size("tp")
    slots = base_ref.shape[0]
    resident = own_length_ref.shape[0]
    steps = 4
    block = PER_OWNER * steps
    rank = 64
    me = lax.axis_index("pool")
    row = lax.axis_index("tp")
    z_chips = Z_CHIPS
    x_chips = groups // (z_chips * CORES)
    my_x, my_z, my_core = me // (z_chips * CORES), (me // CORES) % z_chips, me % CORES

    chunk = 2 * x_chips * CORES
    chunks = groups // chunk
    turns = sorted(range(x_chips), key=lambda x: -min(x, x_chips - x))
    last, self_m = chunks - 1, chunk - CORES
    self_k = last * chunk + self_m
    ahead = [lax.rem(my_x + x, x_chips) * (z_chips * CORES) for x in turns]
    behind = [lax.rem(my_x + (x_chips - x), x_chips) * (z_chips * CORES) for x in turns]
    cores = [my_core, 1 - my_core]

    def partners(c, sign):
        offsets = (z_chips // 2 + c, z_chips // 2 - 1 - c)
        to_z = [
            lax.rem(my_z + (z if sign > 0 else z_chips - z), z_chips) * CORES for z in offsets
        ]
        return [
            to_x + z + core
            for z in to_z
            for to_x in (ahead if sign > 0 else behind)
            for core in cores
        ]

    def to_chunk(c, sign, send):
        for m, to in enumerate(partners(c, sign)):
            if m == self_m:

                @pl.when(c != last)
                def _():
                    send(c * chunk + m, to)
            else:
                send(c * chunk + m, to)

    def to_all(sign, send):
        @pl.loop(0, chunks)
        def _(c):
            to_chunk(c, sign, functools.partial(send, c))

    loads = [
        pltpu.make_async_copy(source, target, load_sem.at[n])
        for n, (source, target) in enumerate(
            [
                (request_hbm, request_ref),
                (store_row_hbm, store_row_ref),
                (tokens_hbm, tokens_ref),
                (target_hbm, target_ref),
                (length_hbm, length_ref),
                (table_hbm, table_ref),
                (own_length_hbm, own_length_ref),
                (own_table_hbm, own_table_ref),
                (shrink_hbm, shrink_ref),
                (expand_hbm, expand_ref),
                (base_hbm, base_ref),
                (fresh_hbm, fresh_ref),
                (pages_hbm, pages_ref),
                (own_pages_hbm, own_pages_ref),
            ]
        )
    ]
    for load in loads:
        load.start()

    barrier = pltpu.get_barrier_semaphore()

    def greet(c, k, to):
        pl.semaphore_signal(barrier, inc=1, device_id={"pool": to}, device_id_type=MESH)

    to_all(1, greet)

    @pl.loop(1, peers)
    def _(j):
        pl.semaphore_signal(
            barrier, inc=1, device_id={"tp": lax.rem(row + j, peers)}, device_id_type=MESH
        )

    for load in loads[:3]:
        load.wait()

    stored = shrink_ref.shape[0] // rank
    adapters = store_row_ref.shape[1]
    store_row = store_row_ref[...]
    request = request_ref[...]
    half = lax.broadcasted_iota(jnp.int32, (8, adapters), 0)
    parts = jnp.where(half == 0, store_row // stored, store_row % stored)
    named = lax.broadcasted_iota(jnp.int32, (adapters, slots), 0) == request
    found = jnp.dot(
        parts.astype(jnp.float32).astype(jnp.bfloat16),
        jnp.where(named, 1.0, 0.0).astype(jnp.bfloat16),
        preferred_element_type=jnp.float32,
    )
    holder, within = found[0:1], found[1:2]
    slot_row = lax.broadcasted_iota(jnp.int32, (slots, slots), 0)
    slot_col = lax.broadcasted_iota(jnp.int32, (slots, slots), 1)
    holder_col = jnp.sum(
        jnp.where(slot_row == slot_col, holder, 0.0), axis=1, keepdims=True
    )
    earlier = (holder_col == holder) & (slot_row < slot_col)
    place = holder * PER_OWNER + jnp.sum(
        jnp.where(earlier, 1.0, 0.0), axis=0, keepdims=True
    )

    holder_ids = lax.broadcasted_iota(jnp.int32, (groups, slots), 0).astype(jnp.float32)
    wanted = jnp.max(jnp.where(holder_ids == holder, within, 0.0), axis=1, keepdims=True)
    pick_send[...] = jnp.broadcast_to(wanted, (groups, HEAD_WIDTH)).reshape(
        groups, 1, HEAD_WIDTH
    )

    wide = slots * steps
    widen = lax.broadcasted_iota(
        jnp.int32, (slots, wide), 1
    ) // steps == lax.broadcasted_iota(jnp.int32, (slots, wide), 0)
    place_wide = jnp.dot(
        jnp.broadcast_to(place, (8, slots)).astype(jnp.bfloat16),
        jnp.where(widen, 1.0, 0.0).astype(jnp.bfloat16),
        preferred_element_type=jnp.float32,
    )[0:1]
    step_of = lax.broadcasted_iota(jnp.int32, (1, wide), 1) % steps
    place_wide = place_wide * steps + step_of.astype(jnp.float32)
    row_ids = lax.broadcasted_iota(jnp.int32, (groups * block, wide), 0).astype(jnp.float32)
    dispatch = jnp.where(row_ids == place_wide, 1.0, 0.0).astype(jnp.bfloat16)
    outgoing = jnp.dot(dispatch, tokens_ref[...], preferred_element_type=jnp.float32)
    x_send[...] = outgoing.reshape(x_send.shape).astype(jnp.bfloat16)

    pl.semaphore_wait(barrier, groups - 1 + peers - 1)

    def send_tokens(c, k, to):
        pltpu.make_async_remote_copy(
            x_send.at[to],
            x_recv.at[k],
            send_sem.at[0],
            x_sem.at[c],
            device_id={"pool": to},
            device_id_type=MESH,
        ).start()
        pltpu.make_async_remote_copy(
            pick_send.at[to],
            pick_recv.at[k],
            send_sem.at[1],
            pick_sem.at[c],
            device_id={"pool": to},
            device_id_type=MESH,
        ).start()

    to_all(-1, send_tokens)

    pltpu.make_async_copy(x_send.at[me], x_recv.at[self_k], x_sem.at[last]).start()
    pltpu.make_async_copy(pick_send.at[me], pick_recv.at[self_k], pick_sem.at[last]).start()

    for load in loads[3:8]:
        load.wait()
    group_lane = lax.broadcasted_iota(jnp.int32, (1, plan_line.shape[1]), 1)

    def assign(j, lines):
        hit = group_lane == target_ref[j]
        found = (table_ref[0, j], table_ref[1, j], length_ref[j])
        return tuple(jnp.where(hit, new, old) for new, old in zip(found, lines))

    empty = jnp.zeros(group_lane.shape, jnp.int32)
    lines = lax.fori_loop(0, target_ref.shape[0], assign, (empty, empty, empty))
    plan_line[...] = jnp.zeros_like(plan_line)
    for n in range(3):
        plan_line[n : n + 1, :] = lines[n]
    plan_copy = pltpu.make_async_copy(plan_line, plan_ref, load_sem.at[len(loads)])
    plan_copy.start()

    span = slots * block
    line = lax.broadcasted_iota(jnp.int32, (span, slots), 0)
    own_line = line // block == lax.broadcasted_iota(jnp.int32, (span, slots), 1)
    holder_line = jnp.sum(jnp.where(own_line, holder, 0.0), axis=1, keepdims=True)
    place_line = jnp.sum(jnp.where(own_line, place, 0.0), axis=1, keepdims=True)
    inner = lax.broadcasted_iota(jnp.int32, (span, 1), 0) % block
    inner = (inner // steps) * block + inner % steps
    source = (
        holder_line * (2 * block)
        + (place_line - holder_line * PER_OWNER) * steps
        + inner.astype(jnp.float32)
    )
    column = lax.broadcasted_iota(jnp.int32, (span, groups * 2 * block), 1)
    gather_ref[...] = jnp.where(column.astype(jnp.float32) == source, 1.0, 0.0).astype(
        jnp.bfloat16
    )

    plan_copy.wait()
    loads[8].wait()
    loads[9].wait()
    lanes = HEAD_WIDTH // rank
    rows = chunk * block
    tiles = stored // lanes
    lane = lax.broadcasted_iota(jnp.int32, (rows, HEAD_WIDTH), 1)
    lane_half = (lane // rank).astype(jnp.float32)
    low_lane = lax.broadcasted_iota(jnp.int32, (rows // 2, HEAD_WIDTH), 1) < rank

    def wait_for(ref, sem):
        pltpu.make_async_copy(ref, ref, sem).wait()

    def picked(c):
        pick = pick_recv[pl.ds(c * chunk, chunk)]
        return jnp.broadcast_to(pick, (chunk, block, HEAD_WIDTH)).reshape(rows, HEAD_WIDTH)

    def shrink_chunk(c):
        here = pl.ds(c * chunk, chunk)
        wait_for(x_recv.at[here], x_sem.at[c])
        wait_for(pick_recv.at[here], pick_sem.at[c])
        x = x_recv[here].reshape(rows, x_recv.shape[2])
        every = lax.dot_general(
            x, shrink_ref[...], (((1,), (1,)), ((), ())), preferred_element_type=jnp.float32
        )
        pick = picked(c)
        low = jnp.zeros((rows, HEAD_WIDTH), jnp.float32)
        for tile in range(tiles):
            part = every[:, tile * HEAD_WIDTH : (tile + 1) * HEAD_WIDTH]
            low += jnp.where(pick == lane_half + tile * lanes, part, 0.0)
        low += pltpu.roll(low, rank, 1)
        part_send[c] = jnp.where(low_lane, low[: rows // 2], low[rows // 2 :]).astype(
            jnp.bfloat16
        )
        pltpu.make_async_copy(
            part_send.at[c], part_recv.at[c, row], part_sem.at[c]
        ).start()

        @pl.loop(1, peers)
        def _(j):
            pltpu.make_async_remote_copy(
                part_send.at[c],
                part_recv.at[c, row],
                send_sem.at[2],
                part_sem.at[c],
                device_id={"tp": lax.rem(row + j, peers)},
                device_id_type=MESH,
            ).start()

    def expand_chunk(c):
        wait_for(part_recv.at[c], part_sem.at[c])
        total = jnp.sum(part_recv[c].astype(jnp.float32), axis=0)
        total = total.astype(jnp.bfloat16).astype(jnp.float32)
        turned = pltpu.roll(total, rank, 1)
        low = jnp.concatenate(
            [jnp.where(low_lane, total, turned), jnp.where(low_lane, turned, total)], 0
        )
        pick = picked(c)
        spread = jnp.concatenate(
            [jnp.where(pick == lane_half + tile * lanes, low, 0.0) for tile in range(tiles)], 1
        ).astype(jnp.bfloat16)
        delta = jnp.dot(spread, expand_ref[...], preferred_element_type=jnp.float32)
        here = pl.ds(c * chunk, chunk)
        for head in range(4):
            piece = delta[:, head * HEAD_WIDTH : (head + 1) * HEAD_WIDTH]
            delta_send[here, head * block : (head + 1) * block, :] = piece.reshape(
                chunk, block, HEAD_WIDTH
            ).astype(jnp.bfloat16)

        def send_delta(k, to):
            pltpu.make_async_remote_copy(
                delta_send.at[k],
                delta_recv.at[me],
                send_sem.at[3],
                one_sem.at[0],
                device_id={"pool": to},
                device_id_type=MESH,
            ).start()

        to_chunk(c, 1, send_delta)

    shrink_chunk(0)

    @pl.loop(1, chunks)
    def _(c):
        shrink_chunk(c)
        expand_chunk(c - 1)

    expand_chunk(chunks - 1)
    pltpu.make_async_copy(delta_send.at[self_k], delta_recv.at[me], one_sem.at[0]).start()

    loads[11].wait()

    def send_fresh(c, k, to):
        pltpu.make_async_remote_copy(
            fresh_ref.at[resident + to],
            fresh_recv.at[k],
            send_sem.at[4],
            one_sem.at[1],
            device_id={"pool": to},
            device_id_type=MESH,
        ).start()

    to_all(-1, send_fresh)

    pltpu.make_async_copy(
        fresh_ref.at[resident + me], fresh_recv.at[self_k], one_sem.at[1]
    ).start()
    loads[10].wait()
    loads[12].wait()
    loads[13].wait()

    wait_for(delta_recv, one_sem.at[0])
    for pair in range(2):
        here = slice(pair * 2 * block, (pair + 1) * 2 * block)
        delta = jnp.dot(
            gather_ref[...],
            delta_recv[:, here, :].reshape(groups * 2 * block, HEAD_WIDTH),
            preferred_element_type=jnp.float32,
        ).reshape(slots, block, HEAD_WIDTH)
        mine = slice(pair * block, (pair + 1) * block)
        query_ref[:, mine, :] = (base_ref[:, mine, :].astype(jnp.float32) + delta).astype(
            jnp.bfloat16
        )

    def send_query(c, k, to):
        pltpu.make_async_remote_copy(
            query_ref.at[resident + to],
            query_recv.at[k],
            send_sem.at[5],
            query_sem.at[c],
            device_id={"pool": to},
            device_id_type=MESH,
        ).start()

    to_all(-1, send_query)

    pltpu.make_async_copy(
        query_ref.at[resident + me], query_recv.at[self_k], query_sem.at[last]
    ).start()

    def attend(number, queries, fresh, slot_pages, slot_length, pool_ref):
        lines = number * 16
        flat = queries.reshape(lines, HEAD_WIDTH)
        new = fresh.reshape(-1, HEAD_WIDTH)
        new_scores = (
            lax.dot_general(
                flat, new, (((1,), (1,)), ((), ())), preferred_element_type=jnp.float32
            )
            * SCALE
        )
        at = lax.broadcasted_iota(jnp.int32, new_scores.shape, 0)
        key = lax.broadcasted_iota(jnp.int32, new_scores.shape, 1)
        seen = (at // 16 == key // 8) & ((key % 8) // 2 <= at % steps) & (key % 2 == 0)
        new_scores = jnp.where(seen, new_scores, -jnp.inf)
        position = lax.broadcasted_iota(jnp.int32, (16, HEAD_WIDTH), 1)
        for m in range(number):
            first, second = slot_pages(m)
            keys = jnp.concatenate([pool_ref[first, 0], pool_ref[second, 0]], 0)
            scores = lax.dot_general(
                queries[m], keys, (((1,), (1,)), ((), ())), preferred_element_type=jnp.float32
            )
            score_ref[m * 16 : (m + 1) * 16, :] = jnp.where(
                position < slot_length(m), scores * SCALE, -jnp.inf
            )
        scores = score_ref[:lines, :]
        highest = jnp.maximum(
            jnp.max(scores, axis=1, keepdims=True), jnp.max(new_scores, axis=1, keepdims=True)
        )
        weights = jnp.exp(scores - highest)
        new_weights = jnp.exp(new_scores - highest)
        total = jnp.sum(weights, axis=1, keepdims=True) + jnp.sum(
            new_weights, axis=1, keepdims=True
        )
        weight_ref[:lines, :] = weights.astype(jnp.bfloat16)
        for m in range(number):
            first, second = slot_pages(m)
            values = jnp.concatenate([pool_ref[first, 1], pool_ref[second, 1]], 0)
            mixed = jnp.dot(
                weight_ref[m * 16 : (m + 1) * 16, :], values, preferred_element_type=jnp.float32
            )
            mix_ref[m * 16 : (m + 1) * 16, :] = jnp.where(slot_length(m) > 0, mixed, 0.0)
        moved = pltpu.roll(new_weights, 1, 1).astype(jnp.bfloat16)
        new_mixed = jnp.dot(moved, new, preferred_element_type=jnp.float32)
        return (mix_ref[:lines, :] + new_mixed) / total

    own = attend(
        resident,
        query_ref[:resident],
        fresh_ref[:FRESH_SLOTS],
        lambda m: (own_table_ref[0, m], own_table_ref[1, m]),
        lambda m: own_length_ref[m],
        own_pages_ref,
    )
    own_mixed[...] = own.reshape(own_mixed.shape).astype(jnp.bfloat16)
    own_copy = pltpu.make_async_copy(own_mixed, out_ref.at[pl.ds(0, resident)], one_sem.at[3])
    own_copy.start()

    wait_for(fresh_recv, one_sem.at[1])

    @pl.loop(0, chunks)
    def _(c):
        here = pl.ds(c * chunk, chunk)
        wait_for(query_recv.at[here], query_sem.at[c])
        at = partners(c, 1)
        mixed = attend(
            chunk,
            query_recv[here],
            fresh_recv[here],
            lambda m: (plan_ref[0, at[m]], plan_ref[1, at[m]]),
            lambda m: plan_ref[2, at[m]],
            pages_ref,
        ).reshape(chunk, 16, HEAD_WIDTH)
        for m in range(chunk):
            mixed_send[c * chunk + m] = jnp.where(plan_ref[2, at[m]] > 0, mixed[m], 0.0).astype(
                jnp.bfloat16
            )

        def send_mixed(k, to):
            pltpu.make_async_remote_copy(
                mixed_send.at[k],
                out_ref.at[resident + me],
                send_sem.at[6],
                one_sem.at[2],
                device_id={"pool": to},
                device_id_type=MESH,
            ).start()

        to_chunk(c, 1, send_mixed)

    pltpu.make_async_copy(
        mixed_send.at[self_k], out_ref.at[resident + me], one_sem.at[2]
    ).start()

    others = pl.ds(0, groups - 1)
    wait_for(x_send.at[others], send_sem.at[0])
    wait_for(pick_send.at[others], send_sem.at[1])
    wait_for(part_recv.at[:, pl.ds(0, peers - 1)], send_sem.at[2])
    wait_for(delta_send.at[others], send_sem.at[3])
    wait_for(fresh_recv.at[others], send_sem.at[4])
    wait_for(query_recv.at[others], send_sem.at[5])
    wait_for(mixed_send.at[others], send_sem.at[6])
    own_copy.wait()
    wait_for(mixed_send, one_sem.at[2])


def body(
    prefill_page_pool,
    prefill_page_table,
    prefill_length,
    prefill_target_group,
    resident_page_pool,
    resident_page_table,
    resident_length,
    tokens,
    base_query_projection,
    fresh_key_value,
    request_adapter,
    adapter_store_row,
    shrink_weight,
    expand_weight,
):
    groups = lax.axis_size("pool")
    peers = lax.axis_size("tp")
    slots, steps, width = tokens.shape
    stored, rank, _ = shrink_weight.shape
    out_width = expand_weight.shape[2]
    heads = out_width // HEAD_WIDTH
    resident = resident_length.shape[0]
    block = PER_OWNER * steps
    lines = heads * steps
    chunk = 2 * groups // Z_CHIPS
    chunks = groups // chunk
    most = max(chunk, resident) * lines

    base = (
        base_query_projection.reshape(slots, steps, heads, HEAD_WIDTH)
        .transpose(0, 2, 1, 3)
        .reshape(slots, lines, HEAD_WIDTH)
    )
    operands = [
        prefill_target_group,
        prefill_length,
        prefill_page_table.T,
        resident_length,
        resident_page_table.T,
        request_adapter.reshape(1, slots),
        adapter_store_row.reshape(1, -1),
        tokens.reshape(slots * steps, width),
        shrink_weight.reshape(stored * rank, width),
        expand_weight.reshape(stored * rank, out_width),
        base,
        fresh_key_value.reshape(slots, 2 * steps, HEAD_WIDTH),
        prefill_page_pool,
        resident_page_pool,
    ]
    hbm = pl.BlockSpec(memory_space=pl.ANY)
    half = jnp.bfloat16
    dma = pltpu.SemaphoreType.DMA
    out = pl.pallas_call(
        kernel,
        out_shape=jax.ShapeDtypeStruct((slots, lines, HEAD_WIDTH), half),
        in_specs=[hbm] * len(operands),
        out_specs=hbm,
        scratch_shapes=[
            pltpu.SMEM(operand.shape, operand.dtype) for operand in operands[:5]
        ]
        + [pltpu.VMEM(operand.shape, operand.dtype) for operand in operands[5:]]
        + [pltpu.VMEM((8, HEAD_WIDTH), jnp.int32), pltpu.SMEM((8, HEAD_WIDTH), jnp.int32)]
        + [
            pltpu.VMEM((slots * block, groups * 2 * block), half),
            pltpu.VMEM((groups, block, width), half),
            pltpu.VMEM((groups, block, width), half),
            pltpu.VMEM((groups, 1, HEAD_WIDTH), jnp.float32),
            pltpu.VMEM((groups, 1, HEAD_WIDTH), jnp.float32),
            pltpu.VMEM((chunks, chunk * block // 2, HEAD_WIDTH), half),
            pltpu.VMEM((chunks, peers, chunk * block // 2, HEAD_WIDTH), half),
            pltpu.VMEM((groups, heads * block, HEAD_WIDTH), half),
            pltpu.VMEM((groups, heads * block, HEAD_WIDTH), half),
            pltpu.VMEM((groups, 2 * steps, HEAD_WIDTH), half),
            pltpu.VMEM((slots, lines, HEAD_WIDTH), half),
            pltpu.VMEM((groups, lines, HEAD_WIDTH), half),
            pltpu.VMEM((groups, lines, HEAD_WIDTH), half),
            pltpu.VMEM((resident, lines, HEAD_WIDTH), half),
            pltpu.VMEM((most, HEAD_WIDTH), jnp.float32),
            pltpu.VMEM((most, HEAD_WIDTH), half),
            pltpu.VMEM((most, HEAD_WIDTH), jnp.float32),
            dma((len(operands) + 1,)),
            dma((chunks,)),
            dma((chunks,)),
            dma((chunks,)),
            dma((chunks,)),
            dma((4,)),
            dma((7,)),
        ],
        compiler_params=pltpu.CompilerParams(
            collective_id=0, has_side_effects=True, vmem_limit_bytes=60 * 1024 * 1024
        ),
    )(*operands)
    return (
        out.reshape(slots, heads, steps, HEAD_WIDTH)
        .transpose(0, 2, 1, 3)
        .reshape(slots, steps, out_width)
    )


def solution(mesh):
    return jax.shard_map(
        body,
        mesh=mesh,
        in_specs=(
            P("pool", None, None, "tp"),
            P("pool", None),
            P("pool"),
            P("pool"),
            P("pool", None, None, "tp"),
            P("pool", None),
            P("pool"),
            P("pool", None, "tp"),
            P("pool", None, "tp"),
            P("pool", None, None, "tp"),
            P("pool"),
            P(),
            P("pool", None, "tp"),
            P("pool", None, "tp"),
        ),
        out_specs=P("pool", None, "tp"),
        check_vma=False,
    )
```

```python
import functools

import jax
import jax.numpy as jnp
from jax import lax
from jax.experimental import pallas as pl
from jax.experimental.pallas import tpu as pltpu
from jax.sharding import PartitionSpec as P

HEAD_WIDTH = 128
SCALE = HEAD_WIDTH ** (-0.5)
MESH = pl.DeviceIdType.MESH
PER_OWNER = 2
CORES = 2
Z_CHIPS = 8
FRESH_SLOTS = HEAD_WIDTH // 8


def kernel(
    target_hbm,
    length_hbm,
    table_hbm,
    own_length_hbm,
    own_table_hbm,
    request_hbm,
    store_row_hbm,
    tokens_hbm,
    shrink_hbm,
    expand_hbm,
    base_hbm,
    fresh_hbm,
    pages_hbm,
    own_pages_hbm,
    out_ref,
    target_ref,
    length_ref,
    table_ref,
    own_length_ref,
    own_table_ref,
    request_ref,
    store_row_ref,
    tokens_ref,
    shrink_ref,
    expand_ref,
    base_ref,
    fresh_ref,
    pages_ref,
    own_pages_ref,
    plan_line,
    plan_ref,
    gather_ref,
    x_send,
    x_recv,
    pick_send,
    pick_recv,
    part_send,
    part_recv,
    delta_send,
    delta_recv,
    fresh_recv,
    query_ref,
    query_recv,
    mixed_send,
    own_mixed,
    score_ref,
    weight_ref,
    mix_ref,
    load_sem,
    x_sem,
    pick_sem,
    part_sem,
    query_sem,
    one_sem,
    send_sem,
):
    groups = x_send.shape[0]
    peers = lax.axis_size("tp")
    slots = base_ref.shape[0]
    resident = own_length_ref.shape[0]
    steps = 4
    block = PER_OWNER * steps
    rank = 64
    me = lax.axis_index("pool")
    row = lax.axis_index("tp")
    z_chips = Z_CHIPS
    x_chips = groups // (z_chips * CORES)
    my_x, my_z, my_core = me // (z_chips * CORES), (me // CORES) % z_chips, me % CORES

    chunk = 2 * x_chips * CORES
    chunks = groups // chunk
    turns = sorted(range(x_chips), key=lambda x: -min(x, x_chips - x))
    width = z_chips * CORES
    last, self_m = chunks - 1, chunk - CORES
    self_k = last * chunk + self_m
    ahead = [lax.rem(my_x + x, x_chips) * (z_chips * CORES) for x in turns]
    behind = [lax.rem(my_x + (x_chips - x), x_chips) * (z_chips * CORES) for x in turns]
    cores = [my_core, 1 - my_core]

    def partners(c, sign):
        offsets = (z_chips // 2 + c, z_chips // 2 - 1 - c)
        to_z = [
            lax.rem(my_z + (z if sign > 0 else z_chips - z), z_chips) * CORES for z in offsets
        ]
        return [
            to_x + z + core
            for z in to_z
            for to_x in (ahead if sign > 0 else behind)
            for core in cores
        ]

    wide_turns = [(n + 1) // 2 if n % 2 else (z_chips - n // 2) % z_chips for n in range(z_chips)]

    def columns(c, sign):
        to_x = lax.rem(my_x + (c if sign > 0 else x_chips - c), x_chips) * (z_chips * CORES)
        return [
            to_x + lax.rem(my_z + (z if sign > 0 else z_chips - z), z_chips) * CORES + core
            for z in wide_turns
            for core in cores
        ]

    def to_column(c, sign, send):
        for m, to in enumerate(columns(c, sign)):
            if m == 0:

                @pl.when(c > 0)
                def _():
                    send(c * width, to)
            else:
                send(c * width + m, to)

    def to_chunk(c, sign, send):
        for m, to in enumerate(partners(c, sign)):
            if m == self_m:

                @pl.when(c != last)
                def _():
                    send(c * chunk + m, to)
            else:
                send(c * chunk + m, to)

    def to_all(sign, send):
        @pl.loop(0, chunks)
        def _(c):
            to_chunk(c, sign, functools.partial(send, c))

    loads = [
        pltpu.make_async_copy(source, target, load_sem.at[n])
        for n, (source, target) in enumerate(
            [
                (request_hbm, request_ref),
                (store_row_hbm, store_row_ref),
                (tokens_hbm, tokens_ref),
                (target_hbm, target_ref),
                (length_hbm, length_ref),
                (table_hbm, table_ref),
                (own_length_hbm, own_length_ref),
                (own_table_hbm, own_table_ref),
                (shrink_hbm, shrink_ref),
                (expand_hbm, expand_ref),
                (base_hbm, base_ref),
                (fresh_hbm, fresh_ref),
                (pages_hbm, pages_ref),
                (own_pages_hbm, own_pages_ref),
            ]
        )
    ]
    for load in loads:
        load.start()

    barrier = pltpu.get_barrier_semaphore()

    def greet(c, k, to):
        pl.semaphore_signal(barrier, inc=1, device_id={"pool": to}, device_id_type=MESH)

    to_all(1, greet)

    others_in_row = [
        lax.rem(row + j, peers)
        for j in sorted(range(1, peers), key=lambda j: -min(j, peers - j))
    ]
    for peer in others_in_row:
        pl.semaphore_signal(barrier, inc=1, device_id={"tp": peer}, device_id_type=MESH)

    for load in loads[:3]:
        load.wait()

    stored = shrink_ref.shape[0] // rank
    adapters = store_row_ref.shape[1]
    store_row = store_row_ref[...]
    request = request_ref[...]
    half = lax.broadcasted_iota(jnp.int32, (8, adapters), 0)
    parts = jnp.where(half == 0, store_row // stored, store_row % stored)
    named = lax.broadcasted_iota(jnp.int32, (adapters, slots), 0) == request
    found = jnp.dot(
        parts.astype(jnp.float32).astype(jnp.bfloat16),
        jnp.where(named, 1.0, 0.0).astype(jnp.bfloat16),
        preferred_element_type=jnp.float32,
    )
    holder, within = found[0:1], found[1:2]
    slot_row = lax.broadcasted_iota(jnp.int32, (slots, slots), 0)
    slot_col = lax.broadcasted_iota(jnp.int32, (slots, slots), 1)
    holder_col = jnp.sum(
        jnp.where(slot_row == slot_col, holder, 0.0), axis=1, keepdims=True
    )
    earlier = (holder_col == holder) & (slot_row < slot_col)
    place = holder * PER_OWNER + jnp.sum(
        jnp.where(earlier, 1.0, 0.0), axis=0, keepdims=True
    )

    holder_ids = lax.broadcasted_iota(jnp.int32, (groups, slots), 0).astype(jnp.float32)
    wanted = jnp.max(jnp.where(holder_ids == holder, within, 0.0), axis=1, keepdims=True)
    pick_send[...] = jnp.broadcast_to(wanted, (groups, HEAD_WIDTH)).reshape(
        groups, 1, HEAD_WIDTH
    )

    wide = slots * steps
    widen = lax.broadcasted_iota(
        jnp.int32, (slots, wide), 1
    ) // steps == lax.broadcasted_iota(jnp.int32, (slots, wide), 0)
    place_wide = jnp.dot(
        jnp.broadcast_to(place, (8, slots)).astype(jnp.bfloat16),
        jnp.where(widen, 1.0, 0.0).astype(jnp.bfloat16),
        preferred_element_type=jnp.float32,
    )[0:1]
    step_of = lax.broadcasted_iota(jnp.int32, (1, wide), 1) % steps
    place_wide = place_wide * steps + step_of.astype(jnp.float32)
    row_ids = lax.broadcasted_iota(jnp.int32, (groups * block, wide), 0).astype(jnp.float32)
    dispatch = jnp.where(row_ids == place_wide, 1.0, 0.0).astype(jnp.bfloat16)
    outgoing = jnp.dot(dispatch, tokens_ref[...].reshape(wide, tokens_ref.shape[2]), preferred_element_type=jnp.float32)
    x_send[...] = outgoing.reshape(x_send.shape).astype(jnp.bfloat16)

    pl.semaphore_wait(barrier, groups - 1 + peers - 1)

    def send_tokens(c, k, to):
        pltpu.make_async_remote_copy(
            x_send.at[to],
            x_recv.at[k],
            send_sem.at[0],
            x_sem.at[c],
            device_id={"pool": to},
            device_id_type=MESH,
        ).start()
        pltpu.make_async_remote_copy(
            pick_send.at[to],
            pick_recv.at[k],
            send_sem.at[1],
            pick_sem.at[c],
            device_id={"pool": to},
            device_id_type=MESH,
        ).start()

    @pl.loop(0, x_chips)
    def _(c):
        to_column(c, -1, functools.partial(send_tokens, c))

    pltpu.make_async_copy(x_send.at[me], x_recv.at[0], x_sem.at[0]).start()
    pltpu.make_async_copy(pick_send.at[me], pick_recv.at[0], pick_sem.at[0]).start()

    loads[11].wait()

    def send_fresh(c, k, to):
        pltpu.make_async_remote_copy(
            fresh_ref.at[resident + to],
            fresh_recv.at[k],
            send_sem.at[4],
            one_sem.at[1],
            device_id={"pool": to},
            device_id_type=MESH,
        ).start()

    to_all(-1, send_fresh)

    pltpu.make_async_copy(
        fresh_ref.at[resident + me], fresh_recv.at[self_k], one_sem.at[1]
    ).start()
    for load in loads[3:8]:
        load.wait()
    group_lane = lax.broadcasted_iota(jnp.int32, (1, plan_line.shape[1]), 1)

    def assign(j, lines):
        hit = group_lane == target_ref[j]
        found = (table_ref[0, j], table_ref[1, j], length_ref[j])
        return tuple(jnp.where(hit, new, old) for new, old in zip(found, lines))

    empty = jnp.zeros(group_lane.shape, jnp.int32)
    lines = lax.fori_loop(0, target_ref.shape[0], assign, (empty, empty, empty))
    plan_line[...] = jnp.zeros_like(plan_line)
    for n in range(3):
        plan_line[n : n + 1, :] = lines[n]
    plan_copy = pltpu.make_async_copy(plan_line, plan_ref, load_sem.at[len(loads)])
    plan_copy.start()

    span = slots * block
    line = lax.broadcasted_iota(jnp.int32, (span, slots), 0)
    own_line = line // block == lax.broadcasted_iota(jnp.int32, (span, slots), 1)
    holder_line = jnp.sum(jnp.where(own_line, holder, 0.0), axis=1, keepdims=True)
    place_line = jnp.sum(jnp.where(own_line, place, 0.0), axis=1, keepdims=True)
    inner = lax.broadcasted_iota(jnp.int32, (span, 1), 0) % block
    inner = (inner // steps) * block + inner % steps
    source = (
        holder_line * (2 * block)
        + (place_line - holder_line * PER_OWNER) * steps
        + inner.astype(jnp.float32)
    )
    column = lax.broadcasted_iota(jnp.int32, (span, groups * 2 * block), 1)
    gather_ref[...] = jnp.where(column.astype(jnp.float32) == source, 1.0, 0.0).astype(
        jnp.bfloat16
    )

    plan_copy.wait()
    loads[8].wait()
    loads[9].wait()
    lanes = HEAD_WIDTH // rank
    rows = width * block
    tiles = stored // lanes
    lane = lax.broadcasted_iota(jnp.int32, (rows, HEAD_WIDTH), 1)
    lane_half = (lane // rank).astype(jnp.float32)
    low_lane = lax.broadcasted_iota(jnp.int32, (rows // 2, HEAD_WIDTH), 1) < rank

    def wait_for(ref, sem):
        pltpu.make_async_copy(ref, ref, sem).wait()

    def picked(c):
        pick = pick_recv[pl.ds(c * width, width)]
        return jnp.broadcast_to(pick, (width, block, HEAD_WIDTH)).reshape(rows, HEAD_WIDTH)

    def shrink_chunk(c):
        here = pl.ds(c * width, width)
        wait_for(x_recv.at[here], x_sem.at[c])
        wait_for(pick_recv.at[here], pick_sem.at[c])
        x = x_recv[here].reshape(rows, x_recv.shape[2])
        every = lax.dot_general(
            x, shrink_ref[...], (((1,), (1,)), ((), ())), preferred_element_type=jnp.float32
        )
        pick = picked(c)
        low = jnp.zeros((rows, HEAD_WIDTH), jnp.float32)
        for tile in range(tiles):
            part = every[:, tile * HEAD_WIDTH : (tile + 1) * HEAD_WIDTH]
            low += jnp.where(pick == lane_half + tile * lanes, part, 0.0)
        low += pltpu.roll(low, rank, 1)
        part_send[c] = jnp.where(low_lane, low[: rows // 2], low[rows // 2 :]).astype(
            jnp.bfloat16
        )
        pltpu.make_async_copy(
            part_send.at[c], part_recv.at[c, row], part_sem.at[c]
        ).start()

        for peer in others_in_row:
            pltpu.make_async_remote_copy(
                part_send.at[c],
                part_recv.at[c, row],
                send_sem.at[2],
                part_sem.at[c],
                device_id={"tp": peer},
                device_id_type=MESH,
            ).start()

    def expand_chunk(c):
        wait_for(part_recv.at[c], part_sem.at[c])
        total = jnp.sum(part_recv[c].astype(jnp.float32), axis=0)
        total = total.astype(jnp.bfloat16).astype(jnp.float32)
        turned = pltpu.roll(total, rank, 1)
        low = jnp.concatenate(
            [jnp.where(low_lane, total, turned), jnp.where(low_lane, turned, total)], 0
        )
        pick = picked(c)
        spread = jnp.concatenate(
            [jnp.where(pick == lane_half + tile * lanes, low, 0.0) for tile in range(tiles)], 1
        ).astype(jnp.bfloat16)
        delta = jnp.dot(spread, expand_ref[...], preferred_element_type=jnp.float32)
        here = pl.ds(c * width, width)
        for head in range(4):
            piece = delta[:, head * HEAD_WIDTH : (head + 1) * HEAD_WIDTH]
            delta_send[here, head * block : (head + 1) * block, :] = piece.reshape(
                width, block, HEAD_WIDTH
            ).astype(jnp.bfloat16)

        def send_delta(k, to):
            pltpu.make_async_remote_copy(
                delta_send.at[k],
                delta_recv.at[me],
                send_sem.at[3],
                one_sem.at[0],
                device_id={"pool": to},
                device_id_type=MESH,
            ).start()

        to_column(c, 1, send_delta)

    shrink_chunk(0)

    @pl.loop(1, x_chips)
    def _(c):
        shrink_chunk(c)
        expand_chunk(c - 1)

    expand_chunk(x_chips - 1)
    pltpu.make_async_copy(delta_send.at[0], delta_recv.at[me], one_sem.at[0]).start()

    loads[10].wait()
    loads[12].wait()
    loads[13].wait()

    wait_for(delta_recv, one_sem.at[0])
    for pair in range(2):
        here = slice(pair * 2 * block, (pair + 1) * 2 * block)
        delta = jnp.dot(
            gather_ref[...],
            delta_recv[:, here, :].reshape(groups * 2 * block, HEAD_WIDTH),
            preferred_element_type=jnp.float32,
        ).reshape(slots, block, HEAD_WIDTH)
        mine = slice(pair * block, (pair + 1) * block)
        query_ref[:, mine, :] = (base_ref[:, mine, :].astype(jnp.float32) + delta).astype(
            jnp.bfloat16
        )

    def send_query(c, k, to):
        pltpu.make_async_remote_copy(
            query_ref.at[resident + to],
            query_recv.at[k],
            send_sem.at[5],
            query_sem.at[c],
            device_id={"pool": to},
            device_id_type=MESH,
        ).start()

    to_all(-1, send_query)

    pltpu.make_async_copy(
        query_ref.at[resident + me], query_recv.at[self_k], query_sem.at[last]
    ).start()

    def attend(number, queries, fresh, slot_pages, slot_length, pool_ref):
        lines = number * 16
        flat = queries.reshape(lines, HEAD_WIDTH)
        new = fresh.reshape(-1, HEAD_WIDTH)
        new_scores = (
            lax.dot_general(
                flat, new, (((1,), (1,)), ((), ())), preferred_element_type=jnp.float32
            )
            * SCALE
        )
        at = lax.broadcasted_iota(jnp.int32, new_scores.shape, 0)
        key = lax.broadcasted_iota(jnp.int32, new_scores.shape, 1)
        seen = (at // 16 == key // 8) & ((key % 8) // 2 <= at % steps) & (key % 2 == 0)
        new_scores = jnp.where(seen, new_scores, -jnp.inf)
        position = lax.broadcasted_iota(jnp.int32, (16, HEAD_WIDTH), 1)
        for m in range(number):
            first, second = slot_pages(m)
            keys = jnp.concatenate([pool_ref[first, 0], pool_ref[second, 0]], 0)
            scores = lax.dot_general(
                queries[m], keys, (((1,), (1,)), ((), ())), preferred_element_type=jnp.float32
            )
            score_ref[m * 16 : (m + 1) * 16, :] = jnp.where(
                position < slot_length(m), scores * SCALE, -jnp.inf
            )
        scores = score_ref[:lines, :]
        highest = jnp.maximum(
            jnp.max(scores, axis=1, keepdims=True), jnp.max(new_scores, axis=1, keepdims=True)
        )
        weights = jnp.exp(scores - highest)
        new_weights = jnp.exp(new_scores - highest)
        total = jnp.sum(weights, axis=1, keepdims=True) + jnp.sum(
            new_weights, axis=1, keepdims=True
        )
        weight_ref[:lines, :] = weights.astype(jnp.bfloat16)
        for m in range(number):
            first, second = slot_pages(m)
            values = jnp.concatenate([pool_ref[first, 1], pool_ref[second, 1]], 0)
            mixed = jnp.dot(
                weight_ref[m * 16 : (m + 1) * 16, :], values, preferred_element_type=jnp.float32
            )
            mix_ref[m * 16 : (m + 1) * 16, :] = jnp.where(slot_length(m) > 0, mixed, 0.0)
        moved = pltpu.roll(new_weights, 1, 1).astype(jnp.bfloat16)
        new_mixed = jnp.dot(moved, new, preferred_element_type=jnp.float32)
        return (mix_ref[:lines, :] + new_mixed) / total

    own = attend(
        resident,
        query_ref[:resident],
        fresh_ref[:FRESH_SLOTS],
        lambda m: (own_table_ref[0, m], own_table_ref[1, m]),
        lambda m: own_length_ref[m],
        own_pages_ref,
    )
    own_mixed[...] = own.reshape(own_mixed.shape).astype(jnp.bfloat16)
    own_copy = pltpu.make_async_copy(own_mixed, out_ref.at[pl.ds(0, resident)], one_sem.at[3])
    own_copy.start()

    wait_for(fresh_recv, one_sem.at[1])

    @pl.loop(0, chunks)
    def _(c):
        here = pl.ds(c * chunk, chunk)
        wait_for(query_recv.at[here], query_sem.at[c])
        at = partners(c, 1)
        mixed = attend(
            chunk,
            query_recv[here],
            fresh_recv[here],
            lambda m: (plan_ref[0, at[m]], plan_ref[1, at[m]]),
            lambda m: plan_ref[2, at[m]],
            pages_ref,
        ).reshape(chunk, 16, HEAD_WIDTH)
        for m in range(chunk):
            mixed_send[c * chunk + m] = jnp.where(plan_ref[2, at[m]] > 0, mixed[m], 0.0).astype(
                jnp.bfloat16
            )

        def send_mixed(k, to):
            pltpu.make_async_remote_copy(
                mixed_send.at[k],
                out_ref.at[resident + me],
                send_sem.at[6],
                one_sem.at[2],
                device_id={"pool": to},
                device_id_type=MESH,
            ).start()

        to_chunk(c, 1, send_mixed)

    pltpu.make_async_copy(
        mixed_send.at[self_k], out_ref.at[resident + me], one_sem.at[2]
    ).start()

    others = pl.ds(0, groups - 1)
    wait_for(x_send.at[others], send_sem.at[0])
    wait_for(pick_send.at[others], send_sem.at[1])
    wait_for(part_recv.at[:, pl.ds(0, peers - 1)], send_sem.at[2])
    wait_for(delta_send.at[others], send_sem.at[3])
    wait_for(fresh_recv.at[others], send_sem.at[4])
    wait_for(query_recv.at[others], send_sem.at[5])
    wait_for(mixed_send.at[others], send_sem.at[6])
    own_copy.wait()
    wait_for(mixed_send, one_sem.at[2])


def body(
    prefill_page_pool,
    prefill_page_table,
    prefill_length,
    prefill_target_group,
    resident_page_pool,
    resident_page_table,
    resident_length,
    tokens,
    base_query_projection,
    fresh_key_value,
    request_adapter,
    adapter_store_row,
    shrink_weight,
    expand_weight,
):
    groups = lax.axis_size("pool")
    peers = lax.axis_size("tp")
    slots, steps, width = tokens.shape
    stored, rank, _ = shrink_weight.shape
    out_width = expand_weight.shape[2]
    heads = out_width // HEAD_WIDTH
    resident = resident_length.shape[0]
    block = PER_OWNER * steps
    lines = heads * steps
    chunk = 2 * groups // Z_CHIPS
    chunks = groups // chunk
    columns = groups // (Z_CHIPS * CORES)
    most = max(chunk, resident) * lines

    base = (
        base_query_projection.reshape(slots, steps, heads, HEAD_WIDTH)
        .transpose(0, 2, 1, 3)
        .reshape(slots, lines, HEAD_WIDTH)
    )
    operands = [
        prefill_target_group,
        prefill_length,
        prefill_page_table.T,
        resident_length,
        resident_page_table.T,
        request_adapter.reshape(1, slots),
        adapter_store_row.reshape(1, -1),
        tokens,
        shrink_weight.reshape(stored * rank, width),
        expand_weight.reshape(stored * rank, out_width),
        base,
        fresh_key_value.reshape(slots, 2 * steps, HEAD_WIDTH),
        prefill_page_pool,
        resident_page_pool,
    ]
    hbm = pl.BlockSpec(memory_space=pl.ANY)
    half = jnp.bfloat16
    dma = pltpu.SemaphoreType.DMA
    out = pl.pallas_call(
        kernel,
        out_shape=jax.ShapeDtypeStruct((slots, lines, HEAD_WIDTH), half),
        in_specs=[hbm] * len(operands),
        out_specs=hbm,
        scratch_shapes=[
            pltpu.SMEM(operand.shape, operand.dtype) for operand in operands[:5]
        ]
        + [pltpu.VMEM(operand.shape, operand.dtype) for operand in operands[5:]]
        + [pltpu.VMEM((8, HEAD_WIDTH), jnp.int32), pltpu.SMEM((8, HEAD_WIDTH), jnp.int32)]
        + [
            pltpu.VMEM((slots * block, groups * 2 * block), half),
            pltpu.VMEM((groups, block, width), half),
            pltpu.VMEM((groups, block, width), half),
            pltpu.VMEM((groups, 1, HEAD_WIDTH), jnp.float32),
            pltpu.VMEM((groups, 1, HEAD_WIDTH), jnp.float32),
            pltpu.VMEM((columns, groups // columns * block // 2, HEAD_WIDTH), half),
            pltpu.VMEM((columns, peers, groups // columns * block // 2, HEAD_WIDTH), half),
            pltpu.VMEM((groups, heads * block, HEAD_WIDTH), half),
            pltpu.VMEM((groups, heads * block, HEAD_WIDTH), half),
            pltpu.VMEM((groups, 2 * steps, HEAD_WIDTH), half),
            pltpu.VMEM((slots, lines, HEAD_WIDTH), half),
            pltpu.VMEM((groups, lines, HEAD_WIDTH), half),
            pltpu.VMEM((groups, lines, HEAD_WIDTH), half),
            pltpu.VMEM((resident, lines, HEAD_WIDTH), half),
            pltpu.VMEM((most, HEAD_WIDTH), jnp.float32),
            pltpu.VMEM((most, HEAD_WIDTH), half),
            pltpu.VMEM((most, HEAD_WIDTH), jnp.float32),
            dma((len(operands) + 1,)),
            dma((columns,)),
            dma((columns,)),
            dma((columns,)),
            dma((chunks,)),
            dma((4,)),
            dma((7,)),
        ],
        compiler_params=pltpu.CompilerParams(
            collective_id=0, has_side_effects=True, vmem_limit_bytes=60 * 1024 * 1024
        ),
    )(*operands)
    return (
        out.reshape(slots, heads, steps, HEAD_WIDTH)
        .transpose(0, 2, 1, 3)
        .reshape(slots, steps, out_width)
    )


def solution(mesh):
    return jax.shard_map(
        body,
        mesh=mesh,
        in_specs=(
            P("pool", None, None, "tp"),
            P("pool", None),
            P("pool"),
            P("pool"),
            P("pool", None, None, "tp"),
            P("pool", None),
            P("pool"),
            P("pool", None, "tp"),
            P("pool", None, "tp"),
            P("pool", None, None, "tp"),
            P("pool"),
            P(),
            P("pool", None, "tp"),
            P("pool", None, "tp"),
        ),
        out_specs=P("pool", None, "tp"),
        check_vma=False,
    )
```

```python
import functools

import jax
import jax.numpy as jnp
from jax import lax
from jax.experimental import pallas as pl
from jax.experimental.pallas import tpu as pltpu
from jax.sharding import PartitionSpec as P

HEAD_WIDTH = 128
SCALE = HEAD_WIDTH ** (-0.5)
MESH = pl.DeviceIdType.MESH
PER_OWNER = 2
CORES = 2
Z_CHIPS = 8
FRESH_SLOTS = HEAD_WIDTH // 8


def kernel(
    target_hbm,
    length_hbm,
    table_hbm,
    own_length_hbm,
    own_table_hbm,
    request_hbm,
    store_row_hbm,
    tokens_hbm,
    shrink_hbm,
    expand_hbm,
    base_hbm,
    fresh_hbm,
    pages_hbm,
    own_pages_hbm,
    out_ref,
    target_ref,
    length_ref,
    table_ref,
    own_length_ref,
    own_table_ref,
    request_ref,
    store_row_ref,
    tokens_ref,
    shrink_ref,
    expand_ref,
    base_ref,
    fresh_ref,
    pages_ref,
    own_pages_ref,
    plan_line,
    plan_ref,
    gather_ref,
    x_send,
    x_recv,
    pick_send,
    pick_recv,
    part_send,
    part_recv,
    delta_send,
    delta_recv,
    fresh_recv,
    query_ref,
    query_recv,
    mixed_send,
    own_mixed,
    score_ref,
    weight_ref,
    mix_ref,
    load_sem,
    x_sem,
    pick_sem,
    part_sem,
    query_sem,
    one_sem,
    send_sem,
):
    groups = x_send.shape[0]
    peers = lax.axis_size("tp")
    slots = base_ref.shape[0]
    resident = own_length_ref.shape[0]
    steps = 4
    block = PER_OWNER * steps
    rank = 64
    me = lax.axis_index("pool")
    row = lax.axis_index("tp")
    z_chips = Z_CHIPS
    x_chips = groups // (z_chips * CORES)
    my_x, my_z, my_core = me // (z_chips * CORES), (me // CORES) % z_chips, me % CORES

    chunk = 2 * x_chips * CORES
    chunks = groups // chunk
    turns = sorted(range(x_chips), key=lambda x: -min(x, x_chips - x))
    width = z_chips * CORES
    own_k = (x_chips - 1) * width
    last, self_m = chunks - 1, chunk - CORES
    self_k = last * chunk + self_m
    ahead = [lax.rem(my_x + x, x_chips) * (z_chips * CORES) for x in turns]
    behind = [lax.rem(my_x + (x_chips - x), x_chips) * (z_chips * CORES) for x in turns]
    cores = [my_core, 1 - my_core]

    def partners(c, sign):
        offsets = (z_chips // 2 + c, z_chips // 2 - 1 - c)
        to_z = [
            lax.rem(my_z + (z if sign > 0 else z_chips - z), z_chips) * CORES for z in offsets
        ]
        return [
            to_x + z + core
            for z in to_z
            for to_x in (ahead if sign > 0 else behind)
            for core in cores
        ]

    wide_turns = [0] + sorted(range(1, z_chips), key=lambda z: -min(z, z_chips - z))

    def columns(c, sign):
        x = x_chips - 1 - c
        to_x = lax.rem(my_x + (x if sign > 0 else x_chips - x), x_chips) * (z_chips * CORES)
        return [
            to_x + lax.rem(my_z + (z if sign > 0 else z_chips - z), z_chips) * CORES + core
            for z in wide_turns
            for core in cores
        ]

    def to_column(c, sign, send):
        for m, to in enumerate(columns(c, sign)):
            if m == 0:

                @pl.when(c < x_chips - 1)
                def _():
                    send(c * width, to)
            else:
                send(c * width + m, to)

    def to_chunk(c, sign, send):
        for m, to in enumerate(partners(c, sign)):
            if m == self_m:

                @pl.when(c != last)
                def _():
                    send(c * chunk + m, to)
            else:
                send(c * chunk + m, to)

    def to_all(sign, send):
        @pl.loop(0, chunks)
        def _(c):
            to_chunk(c, sign, functools.partial(send, c))

    barrier = pltpu.get_barrier_semaphore()

    def greet(c, k, to):
        pl.semaphore_signal(barrier, inc=1, device_id={"pool": to}, device_id_type=MESH)

    to_all(1, greet)

    others_in_row = [
        lax.rem(row + j, peers)
        for j in sorted(range(1, peers), key=lambda j: -min(j, peers - j))
    ]
    for peer in others_in_row:
        pl.semaphore_signal(barrier, inc=1, device_id={"tp": peer}, device_id_type=MESH)

    loads = [
        pltpu.make_async_copy(source, target, load_sem.at[n])
        for n, (source, target) in enumerate(
            [
                (request_hbm, request_ref),
                (store_row_hbm, store_row_ref),
                (tokens_hbm, tokens_ref),
                (target_hbm, target_ref),
                (length_hbm, length_ref),
                (table_hbm, table_ref),
                (own_length_hbm, own_length_ref),
                (own_table_hbm, own_table_ref),
                (shrink_hbm, shrink_ref),
                (expand_hbm, expand_ref),
                (base_hbm, base_ref),
                (fresh_hbm, fresh_ref),
                (pages_hbm, pages_ref),
                (own_pages_hbm, own_pages_ref),
            ]
        )
    ]
    for load in loads:
        load.start()

    for load in loads[:3]:
        load.wait()

    stored = shrink_ref.shape[0] // rank
    adapters = store_row_ref.shape[1]
    store_row = store_row_ref[...]
    request = request_ref[...]
    half = lax.broadcasted_iota(jnp.int32, (8, adapters), 0)
    parts = jnp.where(half == 0, store_row // stored, store_row % stored)
    named = lax.broadcasted_iota(jnp.int32, (adapters, slots), 0) == request
    found = jnp.dot(
        parts.astype(jnp.float32).astype(jnp.bfloat16),
        jnp.where(named, 1.0, 0.0).astype(jnp.bfloat16),
        preferred_element_type=jnp.float32,
    )
    holder, within = found[0:1], found[1:2]
    slot_row = lax.broadcasted_iota(jnp.int32, (slots, slots), 0)
    slot_col = lax.broadcasted_iota(jnp.int32, (slots, slots), 1)
    holder_col = jnp.sum(
        jnp.where(slot_row == slot_col, holder, 0.0), axis=1, keepdims=True
    )
    earlier = (holder_col == holder) & (slot_row < slot_col)
    place = holder * PER_OWNER + jnp.sum(
        jnp.where(earlier, 1.0, 0.0), axis=0, keepdims=True
    )

    holder_ids = lax.broadcasted_iota(jnp.int32, (groups, slots), 0).astype(jnp.float32)
    wanted = jnp.max(jnp.where(holder_ids == holder, within, 0.0), axis=1, keepdims=True)
    pick_send[...] = jnp.broadcast_to(wanted, (groups, HEAD_WIDTH)).reshape(
        groups, 1, HEAD_WIDTH
    )

    wide = slots * steps
    widen = lax.broadcasted_iota(
        jnp.int32, (slots, wide), 1
    ) // steps == lax.broadcasted_iota(jnp.int32, (slots, wide), 0)
    place_wide = jnp.dot(
        jnp.broadcast_to(place, (8, slots)).astype(jnp.bfloat16),
        jnp.where(widen, 1.0, 0.0).astype(jnp.bfloat16),
        preferred_element_type=jnp.float32,
    )[0:1]
    step_of = lax.broadcasted_iota(jnp.int32, (1, wide), 1) % steps
    place_wide = place_wide * steps + step_of.astype(jnp.float32)
    row_ids = lax.broadcasted_iota(jnp.int32, (groups * block, wide), 0).astype(jnp.float32)
    dispatch = jnp.where(row_ids == place_wide, 1.0, 0.0).astype(jnp.bfloat16)
    outgoing = jnp.dot(dispatch, tokens_ref[...].reshape(wide, tokens_ref.shape[2]), preferred_element_type=jnp.float32)
    x_send[...] = outgoing.reshape(x_send.shape).astype(jnp.bfloat16)

    pl.semaphore_wait(barrier, groups - 1 + peers - 1)

    def send_tokens(c, k, to):
        pltpu.make_async_remote_copy(
            x_send.at[to],
            x_recv.at[k],
            send_sem.at[0],
            x_sem.at[c],
            device_id={"pool": to},
            device_id_type=MESH,
        ).start()
        pltpu.make_async_remote_copy(
            pick_send.at[to],
            pick_recv.at[k],
            send_sem.at[1],
            pick_sem.at[c],
            device_id={"pool": to},
            device_id_type=MESH,
        ).start()

    @pl.loop(0, x_chips)
    def _(c):
        to_column(c, -1, functools.partial(send_tokens, c))

    pltpu.make_async_copy(x_send.at[me], x_recv.at[own_k], x_sem.at[x_chips - 1]).start()
    pltpu.make_async_copy(pick_send.at[me], pick_recv.at[own_k], pick_sem.at[x_chips - 1]).start()

    loads[11].wait()

    def send_fresh(c, k, to):
        pltpu.make_async_remote_copy(
            fresh_ref.at[resident + to],
            fresh_recv.at[k],
            send_sem.at[4],
            one_sem.at[1],
            device_id={"pool": to},
            device_id_type=MESH,
        ).start()

    to_all(-1, send_fresh)

    pltpu.make_async_copy(
        fresh_ref.at[resident + me], fresh_recv.at[self_k], one_sem.at[1]
    ).start()
    for load in loads[3:8]:
        load.wait()
    group_lane = lax.broadcasted_iota(jnp.int32, (1, plan_line.shape[1]), 1)

    def assign(j, lines):
        hit = group_lane == target_ref[j]
        found = (table_ref[0, j], table_ref[1, j], length_ref[j])
        return tuple(jnp.where(hit, new, old) for new, old in zip(found, lines))

    empty = jnp.zeros(group_lane.shape, jnp.int32)
    lines = lax.fori_loop(0, target_ref.shape[0], assign, (empty, empty, empty))
    plan_line[...] = jnp.zeros_like(plan_line)
    for n in range(3):
        plan_line[n : n + 1, :] = lines[n]
    plan_copy = pltpu.make_async_copy(plan_line, plan_ref, load_sem.at[len(loads)])
    plan_copy.start()

    span = slots * block
    line = lax.broadcasted_iota(jnp.int32, (span, slots), 0)
    own_line = line // block == lax.broadcasted_iota(jnp.int32, (span, slots), 1)
    holder_line = jnp.sum(jnp.where(own_line, holder, 0.0), axis=1, keepdims=True)
    place_line = jnp.sum(jnp.where(own_line, place, 0.0), axis=1, keepdims=True)
    inner = lax.broadcasted_iota(jnp.int32, (span, 1), 0) % block
    inner = (inner // steps) * block + inner % steps
    source = (
        holder_line * (2 * block)
        + (place_line - holder_line * PER_OWNER) * steps
        + inner.astype(jnp.float32)
    )
    column = lax.broadcasted_iota(jnp.int32, (span, groups * 2 * block), 1)
    gather_ref[...] = jnp.where(column.astype(jnp.float32) == source, 1.0, 0.0).astype(
        jnp.bfloat16
    )

    plan_copy.wait()
    loads[8].wait()
    loads[9].wait()
    lanes = HEAD_WIDTH // rank
    rows = width * block
    tiles = stored // lanes
    lane = lax.broadcasted_iota(jnp.int32, (rows, HEAD_WIDTH), 1)
    lane_half = (lane // rank).astype(jnp.float32)
    low_lane = lax.broadcasted_iota(jnp.int32, (rows // 2, HEAD_WIDTH), 1) < rank

    def wait_for(ref, sem):
        pltpu.make_async_copy(ref, ref, sem).wait()

    def picked(c):
        pick = pick_recv[pl.ds(c * width, width)]
        return jnp.broadcast_to(pick, (width, block, HEAD_WIDTH)).reshape(rows, HEAD_WIDTH)

    def shrink_chunk(c):
        here = pl.ds(c * width, width)
        wait_for(x_recv.at[here], x_sem.at[c])
        wait_for(pick_recv.at[here], pick_sem.at[c])
        x = x_recv[here].reshape(rows, x_recv.shape[2])
        every = lax.dot_general(
            x, shrink_ref[...], (((1,), (1,)), ((), ())), preferred_element_type=jnp.float32
        )
        pick = picked(c)
        low = jnp.zeros((rows, HEAD_WIDTH), jnp.float32)
        for tile in range(tiles):
            part = every[:, tile * HEAD_WIDTH : (tile + 1) * HEAD_WIDTH]
            low += jnp.where(pick == lane_half + tile * lanes, part, 0.0)
        low += pltpu.roll(low, rank, 1)
        part_send[c] = jnp.where(low_lane, low[: rows // 2], low[rows // 2 :]).astype(
            jnp.bfloat16
        )
        pltpu.make_async_copy(
            part_send.at[c], part_recv.at[c, row], part_sem.at[c]
        ).start()

        for peer in others_in_row:
            pltpu.make_async_remote_copy(
                part_send.at[c],
                part_recv.at[c, row],
                send_sem.at[2],
                part_sem.at[c],
                device_id={"tp": peer},
                device_id_type=MESH,
            ).start()

    def expand_chunk(c):
        wait_for(part_recv.at[c], part_sem.at[c])
        total = jnp.sum(part_recv[c].astype(jnp.float32), axis=0)
        total = total.astype(jnp.bfloat16).astype(jnp.float32)
        turned = pltpu.roll(total, rank, 1)
        low = jnp.concatenate(
            [jnp.where(low_lane, total, turned), jnp.where(low_lane, turned, total)], 0
        )
        pick = picked(c)
        spread = jnp.concatenate(
            [jnp.where(pick == lane_half + tile * lanes, low, 0.0) for tile in range(tiles)], 1
        ).astype(jnp.bfloat16)
        delta = jnp.dot(spread, expand_ref[...], preferred_element_type=jnp.float32)
        here = pl.ds(c * width, width)
        for head in range(4):
            piece = delta[:, head * HEAD_WIDTH : (head + 1) * HEAD_WIDTH]
            delta_send[here, head * block : (head + 1) * block, :] = piece.reshape(
                width, block, HEAD_WIDTH
            ).astype(jnp.bfloat16)

        def send_delta(k, to):
            pltpu.make_async_remote_copy(
                delta_send.at[k],
                delta_recv.at[me],
                send_sem.at[3],
                one_sem.at[0],
                device_id={"pool": to},
                device_id_type=MESH,
            ).start()

        to_column(c, 1, send_delta)

    shrink_chunk(0)

    @pl.loop(1, x_chips)
    def _(c):
        shrink_chunk(c)
        expand_chunk(c - 1)

    expand_chunk(x_chips - 1)
    pltpu.make_async_copy(delta_send.at[own_k], delta_recv.at[me], one_sem.at[0]).start()

    loads[10].wait()
    loads[12].wait()
    loads[13].wait()

    wait_for(delta_recv, one_sem.at[0])
    for pair in range(2):
        here = slice(pair * 2 * block, (pair + 1) * 2 * block)
        delta = jnp.dot(
            gather_ref[...],
            delta_recv[:, here, :].reshape(groups * 2 * block, HEAD_WIDTH),
            preferred_element_type=jnp.float32,
        ).reshape(slots, block, HEAD_WIDTH)
        mine = slice(pair * block, (pair + 1) * block)
        query_ref[:, mine, :] = (base_ref[:, mine, :].astype(jnp.float32) + delta).astype(
            jnp.bfloat16
        )

    def send_query(c, k, to):
        pltpu.make_async_remote_copy(
            query_ref.at[resident + to],
            query_recv.at[k],
            send_sem.at[5],
            query_sem.at[c],
            device_id={"pool": to},
            device_id_type=MESH,
        ).start()

    to_all(-1, send_query)

    pltpu.make_async_copy(
        query_ref.at[resident + me], query_recv.at[self_k], query_sem.at[last]
    ).start()

    def attend(number, queries, fresh, slot_pages, slot_length, pool_ref):
        lines = number * 16
        flat = queries.reshape(lines, HEAD_WIDTH)
        new = fresh.reshape(-1, HEAD_WIDTH)
        new_scores = (
            lax.dot_general(
                flat, new, (((1,), (1,)), ((), ())), preferred_element_type=jnp.float32
            )
            * SCALE
        )
        at = lax.broadcasted_iota(jnp.int32, new_scores.shape, 0)
        key = lax.broadcasted_iota(jnp.int32, new_scores.shape, 1)
        seen = (at // 16 == key // 8) & ((key % 8) // 2 <= at % steps) & (key % 2 == 0)
        new_scores = jnp.where(seen, new_scores, -jnp.inf)
        position = lax.broadcasted_iota(jnp.int32, (16, HEAD_WIDTH), 1)
        for m in range(number):
            first, second = slot_pages(m)
            keys = jnp.concatenate([pool_ref[first, 0], pool_ref[second, 0]], 0)
            scores = lax.dot_general(
                queries[m], keys, (((1,), (1,)), ((), ())), preferred_element_type=jnp.float32
            )
            score_ref[m * 16 : (m + 1) * 16, :] = jnp.where(
                position < slot_length(m), scores * SCALE, -jnp.inf
            )
        scores = score_ref[:lines, :]
        highest = jnp.maximum(
            jnp.max(scores, axis=1, keepdims=True), jnp.max(new_scores, axis=1, keepdims=True)
        )
        weights = jnp.exp(scores - highest)
        new_weights = jnp.exp(new_scores - highest)
        total = jnp.sum(weights, axis=1, keepdims=True) + jnp.sum(
            new_weights, axis=1, keepdims=True
        )
        weight_ref[:lines, :] = weights.astype(jnp.bfloat16)
        for m in range(number):
            first, second = slot_pages(m)
            values = jnp.concatenate([pool_ref[first, 1], pool_ref[second, 1]], 0)
            mixed = jnp.dot(
                weight_ref[m * 16 : (m + 1) * 16, :], values, preferred_element_type=jnp.float32
            )
            mix_ref[m * 16 : (m + 1) * 16, :] = jnp.where(slot_length(m) > 0, mixed, 0.0)
        moved = pltpu.roll(new_weights, 1, 1).astype(jnp.bfloat16)
        new_mixed = jnp.dot(moved, new, preferred_element_type=jnp.float32)
        return (mix_ref[:lines, :] + new_mixed) / total

    own = attend(
        resident,
        query_ref[:resident],
        fresh_ref[:FRESH_SLOTS],
        lambda m: (own_table_ref[0, m], own_table_ref[1, m]),
        lambda m: own_length_ref[m],
        own_pages_ref,
    )
    own_mixed[...] = own.reshape(own_mixed.shape).astype(jnp.bfloat16)
    own_copy = pltpu.make_async_copy(own_mixed, out_ref.at[pl.ds(0, resident)], one_sem.at[3])
    own_copy.start()

    wait_for(fresh_recv, one_sem.at[1])

    @pl.loop(0, chunks)
    def _(c):
        here = pl.ds(c * chunk, chunk)
        wait_for(query_recv.at[here], query_sem.at[c])
        at = partners(c, 1)
        mixed = attend(
            chunk,
            query_recv[here],
            fresh_recv[here],
            lambda m: (plan_ref[0, at[m]], plan_ref[1, at[m]]),
            lambda m: plan_ref[2, at[m]],
            pages_ref,
        ).reshape(chunk, 16, HEAD_WIDTH)
        for m in range(chunk):
            mixed_send[c * chunk + m] = jnp.where(plan_ref[2, at[m]] > 0, mixed[m], 0.0).astype(
                jnp.bfloat16
            )

        def send_mixed(k, to):
            pltpu.make_async_remote_copy(
                mixed_send.at[k],
                out_ref.at[resident + me],
                send_sem.at[6],
                one_sem.at[2],
                device_id={"pool": to},
                device_id_type=MESH,
            ).start()

        to_chunk(c, 1, send_mixed)

    pltpu.make_async_copy(
        mixed_send.at[self_k], out_ref.at[resident + me], one_sem.at[2]
    ).start()

    others = pl.ds(0, groups - 1)
    wait_for(x_send.at[others], send_sem.at[0])
    wait_for(pick_send.at[others], send_sem.at[1])
    wait_for(part_recv.at[:, pl.ds(0, peers - 1)], send_sem.at[2])
    wait_for(delta_send.at[others], send_sem.at[3])
    wait_for(fresh_recv.at[others], send_sem.at[4])
    wait_for(query_recv.at[others], send_sem.at[5])
    wait_for(mixed_send.at[others], send_sem.at[6])
    own_copy.wait()
    wait_for(mixed_send, one_sem.at[2])


def body(
    prefill_page_pool,
    prefill_page_table,
    prefill_length,
    prefill_target_group,
    resident_page_pool,
    resident_page_table,
    resident_length,
    tokens,
    base_query_projection,
    fresh_key_value,
    request_adapter,
    adapter_store_row,
    shrink_weight,
    expand_weight,
):
    groups = lax.axis_size("pool")
    peers = lax.axis_size("tp")
    slots, steps, width = tokens.shape
    stored, rank, _ = shrink_weight.shape
    out_width = expand_weight.shape[2]
    heads = out_width // HEAD_WIDTH
    resident = resident_length.shape[0]
    block = PER_OWNER * steps
    lines = heads * steps
    chunk = 2 * groups // Z_CHIPS
    chunks = groups // chunk
    columns = groups // (Z_CHIPS * CORES)
    most = max(chunk, resident) * lines

    base = (
        base_query_projection.reshape(slots, steps, heads, HEAD_WIDTH)
        .transpose(0, 2, 1, 3)
        .reshape(slots, lines, HEAD_WIDTH)
    )
    operands = [
        prefill_target_group,
        prefill_length,
        prefill_page_table.T,
        resident_length,
        resident_page_table.T,
        request_adapter.reshape(1, slots),
        adapter_store_row.reshape(1, -1),
        tokens,
        shrink_weight.reshape(stored * rank, width),
        expand_weight.reshape(stored * rank, out_width),
        base,
        fresh_key_value.reshape(slots, 2 * steps, HEAD_WIDTH),
        prefill_page_pool,
        resident_page_pool,
    ]
    hbm = pl.BlockSpec(memory_space=pl.ANY)
    half = jnp.bfloat16
    dma = pltpu.SemaphoreType.DMA
    out = pl.pallas_call(
        kernel,
        out_shape=jax.ShapeDtypeStruct((slots, lines, HEAD_WIDTH), half),
        in_specs=[hbm] * len(operands),
        out_specs=hbm,
        scratch_shapes=[
            pltpu.SMEM(operand.shape, operand.dtype) for operand in operands[:5]
        ]
        + [pltpu.VMEM(operand.shape, operand.dtype) for operand in operands[5:]]
        + [pltpu.VMEM((8, HEAD_WIDTH), jnp.int32), pltpu.SMEM((8, HEAD_WIDTH), jnp.int32)]
        + [
            pltpu.VMEM((slots * block, groups * 2 * block), half),
            pltpu.VMEM((groups, block, width), half),
            pltpu.VMEM((groups, block, width), half),
            pltpu.VMEM((groups, 1, HEAD_WIDTH), jnp.float32),
            pltpu.VMEM((groups, 1, HEAD_WIDTH), jnp.float32),
            pltpu.VMEM((columns, groups // columns * block // 2, HEAD_WIDTH), half),
            pltpu.VMEM((columns, peers, groups // columns * block // 2, HEAD_WIDTH), half),
            pltpu.VMEM((groups, heads * block, HEAD_WIDTH), half),
            pltpu.VMEM((groups, heads * block, HEAD_WIDTH), half),
            pltpu.VMEM((groups, 2 * steps, HEAD_WIDTH), half),
            pltpu.VMEM((slots, lines, HEAD_WIDTH), half),
            pltpu.VMEM((groups, lines, HEAD_WIDTH), half),
            pltpu.VMEM((groups, lines, HEAD_WIDTH), half),
            pltpu.VMEM((resident, lines, HEAD_WIDTH), half),
            pltpu.VMEM((most, HEAD_WIDTH), jnp.float32),
            pltpu.VMEM((most, HEAD_WIDTH), half),
            pltpu.VMEM((most, HEAD_WIDTH), jnp.float32),
            dma((len(operands) + 1,)),
            dma((columns,)),
            dma((columns,)),
            dma((columns,)),
            dma((chunks,)),
            dma((4,)),
            dma((7,)),
        ],
        compiler_params=pltpu.CompilerParams(
            collective_id=0, has_side_effects=True, vmem_limit_bytes=60 * 1024 * 1024
        ),
    )(*operands)
    return (
        out.reshape(slots, heads, steps, HEAD_WIDTH)
        .transpose(0, 2, 1, 3)
        .reshape(slots, steps, out_width)
    )


def solution(mesh):
    return jax.shard_map(
        body,
        mesh=mesh,
        in_specs=(
            P("pool", None, None, "tp"),
            P("pool", None),
            P("pool"),
            P("pool"),
            P("pool", None, None, "tp"),
            P("pool", None),
            P("pool"),
            P("pool", None, "tp"),
            P("pool", None, "tp"),
            P("pool", None, None, "tp"),
            P("pool"),
            P(),
            P("pool", None, "tp"),
            P("pool", None, "tp"),
        ),
        out_specs=P("pool", None, "tp"),
        check_vma=False,
    )
```
